512 devices in a mesh: dp: 128 (over z, x_lo, y), mp: 4 (over x_hi, core).
Axes of the slice: x: 4 (x_hi: 2, x_lo: 2; x = x_hi * 2 + x_lo), y: 4, z: 16, core: 2. Of those that a mesh axis runs over, the one named last changes fastest.
Arguments:
- img_embed: bfloat16 [49152, 1152], P('dp', 'mp'), may hold values from -6 to 6
- txt_embed: bfloat16 [49152, 1152], P('dp', 'mp'), may hold values from -6 to 6
- img_head: bfloat16 [1152, 1152], P('mp'), may hold values from -0.1875 to 0.1875
- txt_head: bfloat16 [1152, 1152], P('mp'), may hold values from -0.1875 to 0.1875
- pair_ids: int32 [49152], replicated, may hold values from 0 to 24575
Outputs:
- img_grad: bfloat16 [49152, 1152], P('dp', 'mp')
- txt_grad: bfloat16 [49152, 1152], P('dp', 'mp')
- img_head_grad: float32 [1152, 1152], P('mp')
- txt_head_grad: float32 [1152, 1152], P('mp')
The draws below stay inside these ranges and needn't reach their ends.
All inputs are finite; a program needn't handle non-finite values.
Results may differ from the reference program's by a relative error of at most 0.013.
Values may be sent and summed in bfloat16 or wider, within the bound.
No kernel may reach another device: no remote copies, remote signals or barrier semaphores. Data moves between devices by JAX's collectives and lax.ppermute only.
A program may use at most 64 MiB of HBM per device.

```python
import jax
import jax.numpy as jnp
from jax import lax

D = 1152
E = 1152
TOK_DEV = 384
TOKENS = 49152
N_DP = 128


def plant(result, rng, smallest, high):
    spot = [jax.random.randint(jax.random.fold_in(rng, axis), (), 0, length) for axis, length in enumerate(result.shape)]
    longest = result.shape.index(max(result.shape))
    neighbour = spot[:longest] + [(spot[longest] + 1) % result.shape[longest]] + spot[longest + 1:]
    return result.at[tuple(spot)].set(smallest).at[tuple(neighbour)].set(high)


def levels(rng, shape, shards, low, largest):
    level = 1.0
    for axis_at, parts in shards:
        draws = jax.random.uniform(jax.random.fold_in(jax.random.fold_in(rng, 6), axis_at), (parts,), jnp.float32, low / len(shards), largest / len(shards))
        level = level * jnp.repeat(jnp.exp(draws), shape[axis_at] // parts).reshape((-1,) + (1,) * (len(shape) - 1 - axis_at))
    return level


def normal_values(rng, dims, width, limit, cuts=(), held_as=jnp.bfloat16):
    gain = levels(rng, dims, cuts, -0.22, 0.18) if cuts else 1.0
    drawn = jax.random.normal(rng, dims, jnp.float32) * width * gain
    return jnp.minimum(jnp.maximum(drawn, -limit), limit).astype(held_as)


def setup_inputs(seed: int = 0) -> dict:
    seeds = jax.random.split(jax.random.key(seed), 6)
    return {
        "img_embed": normal_values(seeds[0], (TOKENS, D), 1.0, 6.0, ((0, 128), (1, 4))),
        "txt_embed": normal_values(seeds[1], (TOKENS, D), 1.0, 6.0, ((0, 128), (1, 4))),
        "img_head": normal_values(seeds[2], (D, E), D ** -0.5, 0.1875, ((0, 4),)),
        "txt_head": normal_values(seeds[3], (D, E), D ** -0.5, 0.1875, ((0, 4),)),
        "pair_ids": plant(jax.random.randint(seeds[4], (TOKENS,), 0, TOKENS // 2), jax.random.fold_in(seeds[4], 1), 0, (TOKENS // 2) - 1).astype(jnp.int32),
    }


sharpness_multiplier = 10.0
sigmoid_shift_constant = -2.0
loss_scale = 32.0
epsilon = 1e-06

def cosine_agreement_matrix(left, right):
    return jnp.dot(left, right.T, preferred_element_type=jnp.float32)

def signed_labels(left_ids, right_ids):
    return jnp.where(left_ids[:, None] == right_ids[None, :], 1.0, -1.0).astype(jnp.float32)

def pair_grads(matchup_energies, labels):
    return (loss_scale * -labels * jax.nn.sigmoid(-labels * matchup_energies)).astype(jnp.bfloat16)

def reference(img_embed, txt_embed, img_head, txt_head, pair_ids):
    groups = N_DP
    overall_sample_number = TOK_DEV
    half = groups // 2
    img_hid = jnp.dot(img_embed, img_head, preferred_element_type=jnp.float32)
    txt_hid = jnp.dot(txt_embed, txt_head, preferred_element_type=jnp.float32)
    img_norm = jnp.sqrt(lax.optimization_barrier(jnp.sum(img_hid * img_hid, axis=1)) + epsilon)
    txt_norm = jnp.sqrt(lax.optimization_barrier(jnp.sum(txt_hid * txt_hid, axis=1)) + epsilon)
    img_unit = (img_hid / img_norm[:, None]).astype(jnp.bfloat16)
    txt_unit = (txt_hid / txt_norm[:, None]).astype(jnp.bfloat16)
    img_blocks = img_unit.reshape(groups, overall_sample_number, E)
    txt_blocks = txt_unit.reshape(groups, overall_sample_number, E)
    id_blocks = pair_ids.reshape(groups, overall_sample_number)

    def one_block(index):
        far_one = jnp.bitwise_xor(index, half).astype(jnp.int32)
        far_two = jnp.bitwise_xor(index, 1).astype(jnp.int32)
        resident_picture = img_blocks[index]
        resident_caption = txt_blocks[index]
        own_ids = id_blocks[index]
        far_ids = jnp.concatenate([id_blocks[far_one], id_blocks[far_two]])
        normalized_caption_embeddings = jnp.concatenate([resident_caption, txt_blocks[far_one], txt_blocks[far_two]], axis=0)
        faraway_pictures = jnp.concatenate([img_blocks[far_one], img_blocks[far_two]], axis=0)
        leading_energies = sharpness_multiplier * cosine_agreement_matrix(resident_picture, normalized_caption_embeddings) + sigmoid_shift_constant
        spare_match_energies = sharpness_multiplier * cosine_agreement_matrix(resident_caption, faraway_pictures) + sigmoid_shift_constant
        leading_derivatives = pair_grads(leading_energies, signed_labels(own_ids, jnp.concatenate([own_ids, far_ids])))
        extra_grads = pair_grads(spare_match_energies, signed_labels(own_ids, far_ids))
        picture_normed_derivs = sharpness_multiplier * jnp.dot(leading_derivatives, normalized_caption_embeddings, preferred_element_type=jnp.float32)
        resident_share = jnp.dot(leading_derivatives[:, :overall_sample_number].T, resident_picture, preferred_element_type=jnp.float32)
        faraway_share = jnp.dot(extra_grads, faraway_pictures, preferred_element_type=jnp.float32)
        caption_normed_derivs = sharpness_multiplier * (resident_share + faraway_share)
        return (picture_normed_derivs, caption_normed_derivs)
    picture_normed_derivs, caption_normed_derivs = lax.map(one_block, jnp.arange(groups, dtype=jnp.int32))
    picture_normed_derivs = picture_normed_derivs.reshape(groups * overall_sample_number, E)
    caption_normed_derivs = caption_normed_derivs.reshape(groups * overall_sample_number, E)
    img_proj = lax.optimization_barrier(jnp.sum(img_hid * picture_normed_derivs, axis=1))
    txt_proj = lax.optimization_barrier(jnp.sum(txt_hid * caption_normed_derivs, axis=1))
    img_dhid = (picture_normed_derivs / img_norm[:, None] - img_hid * (img_proj / img_norm ** 3)[:, None]).astype(jnp.bfloat16)
    txt_dhid = (caption_normed_derivs / txt_norm[:, None] - txt_hid * (txt_proj / txt_norm ** 3)[:, None]).astype(jnp.bfloat16)
    img_grad = jnp.dot(img_dhid, img_head.T, preferred_element_type=jnp.float32).astype(jnp.bfloat16)
    txt_grad = jnp.dot(txt_dhid, txt_head.T, preferred_element_type=jnp.float32).astype(jnp.bfloat16)
    norm_factor = 1.0 / jnp.sqrt(jnp.float32(groups * overall_sample_number))
    img_head_grad = jnp.dot(img_embed.T, img_dhid, preferred_element_type=jnp.float32) * norm_factor
    txt_head_grad = jnp.dot(txt_embed.T, txt_dhid, preferred_element_type=jnp.float32) * norm_factor
    return (img_grad, txt_grad, img_head_grad, txt_head_grad)
```

```python
import jax
import jax.numpy as jnp
from jax import lax
from jax.sharding import Mesh, PartitionSpec as P

sharpness_multiplier = 10.0
sigmoid_shift_constant = -2.0
loss_scale = 32.0
epsilon = 1e-06
DP = ("z", "xl", "y")
MP = ("xh", "c")
NEAR = ("xl", "y")


def swapped(block, axis, bit):
    count = lax.axis_size(axis)
    return lax.ppermute(block, axis, [(i, i ^ bit) for i in range(count)])


def cosine_agreement_matrix(left, right):
    return jnp.dot(left, right.T, preferred_element_type=jnp.float32)


def signed_labels(left_ids, right_ids):
    return jnp.where(left_ids[:, None] == right_ids[None, :], 1.0, -1.0).astype(jnp.float32)


def pair_grads(matchup_energies, labels):
    return (loss_scale * -labels * jax.nn.sigmoid(-labels * matchup_energies)).astype(jnp.bfloat16)


def summed_over_dp(img_wgrad, txt_wgrad):
    rows, width = img_wgrad.shape
    near = lax.axis_size("xl") * lax.axis_size("y")
    far = lax.axis_size("z")
    both = jnp.concatenate([img_wgrad, txt_wgrad]).astype(jnp.bfloat16)
    share = 2 * rows // near
    parts = lax.all_to_all(both.reshape(near, share, width), NEAR, 0, 0, tiled=True)
    part = jnp.sum(parts.astype(jnp.float32), axis=0)
    tr, tc = share // 8, width // 128
    tiles = part.reshape(tr, 8, tc, 128).transpose(0, 2, 1, 3).reshape(tr * tc, 8, 128)
    each = -(-tr * tc // far)
    tiles = jnp.pad(tiles, ((0, each * far - tr * tc), (0, 0), (0, 0))).astype(jnp.bfloat16)
    pieces = lax.all_to_all(tiles.reshape(far, each * 8, 128), "z", 0, 0, tiled=True)
    piece = jnp.sum(pieces.astype(jnp.float32), axis=0).astype(jnp.bfloat16)
    full = lax.all_gather(piece, "z", axis=0)
    full = full.reshape(each * far, 8, 128)[: tr * tc]
    full = full.reshape(tr, tc, 8, 128).transpose(0, 2, 1, 3).reshape(share, width)
    everyone = lax.all_to_all(
        jnp.broadcast_to(full[None], (near, share, width)), NEAR, 0, 0, tiled=True
    )
    everyone = everyone.reshape(2 * rows, width).astype(jnp.float32)
    return everyone[:rows], everyone[rows:]


def body(img_embed, txt_embed, img_head, txt_head, pair_ids):
    overall_sample_number = img_embed.shape[0]
    groups = lax.axis_size(DP)
    my_group = lax.axis_index(DP)
    img_part = jnp.dot(img_embed, img_head, preferred_element_type=jnp.float32)
    txt_part = jnp.dot(txt_embed, txt_head, preferred_element_type=jnp.float32)
    img_hid, txt_hid = (
        lax.psum_scatter(img_part, MP, scatter_dimension=1, tiled=True),
        lax.psum_scatter(txt_part, MP, scatter_dimension=1, tiled=True),
    )
    img_sq, txt_sq = lax.psum(
        (jnp.sum(img_hid * img_hid, axis=1), jnp.sum(txt_hid * txt_hid, axis=1)), MP
    )
    img_norm = jnp.sqrt(img_sq + epsilon)
    txt_norm = jnp.sqrt(txt_sq + epsilon)
    img_unit = (img_hid / img_norm[:, None]).astype(jnp.bfloat16)
    txt_unit = (txt_hid / txt_norm[:, None]).astype(jnp.bfloat16)
    hops = [(groups // 2, "z", lax.axis_size("z") // 2), (1, "y", 1)]
    own_ids = lax.dynamic_slice_in_dim(
        pair_ids, my_group * overall_sample_number, overall_sample_number
    )
    far_ids = []
    far_txt = []
    for stride, axis, bit in hops:
        partner = jnp.bitwise_xor(my_group, stride)
        far_ids.append(
            lax.dynamic_slice_in_dim(
                pair_ids, partner * overall_sample_number, overall_sample_number
            )
        )
        far_txt.append(swapped(txt_unit, axis, bit))
    col_stack = jnp.stack([txt_unit] + far_txt)
    row_full, col_full = (
        lax.all_gather(img_unit, MP, axis=1, tiled=True),
        lax.all_gather(col_stack, MP, axis=2, tiled=True),
    )
    matchup_energies = cosine_agreement_matrix(row_full, col_full.reshape(-1, col_full.shape[2]))
    matchup_energies = sharpness_multiplier * matchup_energies + sigmoid_shift_constant
    labels = signed_labels(own_ids, jnp.concatenate([own_ids] + far_ids))
    grads = pair_grads(matchup_energies, labels)
    main_width = 3 * overall_sample_number
    shard_width = img_unit.shape[1]
    picture_normed_derivs = sharpness_multiplier * jnp.dot(
        grads, col_stack.reshape(main_width, shard_width), preferred_element_type=jnp.float32
    )
    parcels = jnp.dot(grads.T, img_unit, preferred_element_type=jnp.float32)
    parcels = sharpness_multiplier * parcels.reshape(3, overall_sample_number, shard_width)
    caption_normed_derivs = parcels[0]
    for at, (_, axis, bit) in enumerate(hops):
        caption_normed_derivs = caption_normed_derivs + swapped(
            parcels[at + 1].astype(jnp.bfloat16), axis, bit
        ).astype(jnp.float32)
    img_proj, txt_proj = lax.psum(
        (
            jnp.sum(img_hid * picture_normed_derivs, axis=1),
            jnp.sum(txt_hid * caption_normed_derivs, axis=1),
        ),
        MP,
    )
    img_dhid = (
        picture_normed_derivs / img_norm[:, None] - img_hid * (img_proj / img_norm**3)[:, None]
    ).astype(jnp.bfloat16)
    txt_dhid = (
        caption_normed_derivs / txt_norm[:, None] - txt_hid * (txt_proj / txt_norm**3)[:, None]
    ).astype(jnp.bfloat16)
    img_full, txt_full = (
        lax.all_gather(img_dhid, MP, axis=1, tiled=True),
        lax.all_gather(txt_dhid, MP, axis=1, tiled=True),
    )
    img_grad = jnp.dot(img_full, img_head.T, preferred_element_type=jnp.float32).astype(
        jnp.bfloat16
    )
    txt_grad = jnp.dot(txt_full, txt_head.T, preferred_element_type=jnp.float32).astype(
        jnp.bfloat16
    )
    img_wgrad = jnp.dot(img_embed.T, img_full, preferred_element_type=jnp.float32)
    txt_wgrad = jnp.dot(txt_embed.T, txt_full, preferred_element_type=jnp.float32)
    img_wgrad, txt_wgrad = summed_over_dp(img_wgrad, txt_wgrad)
    norm_factor = 1.0 / jnp.sqrt(jnp.float32(groups * overall_sample_number))
    return (img_grad, txt_grad, img_wgrad * norm_factor, txt_wgrad * norm_factor)


def solution(mesh):
    fine = Mesh(mesh.devices.reshape(16, 2, 4, 2, 2), DP + MP)
    return jax.shard_map(
        body,
        mesh=fine,
        in_specs=(P(DP, MP), P(DP, MP), P(MP, None), P(MP, None), P()),
        out_specs=(P(DP, MP), P(DP, MP), P(MP, None), P(MP, None)),
        check_vma=False,
    )
```

```python
import jax
import jax.numpy as jnp
from jax import lax
from jax.experimental import pallas as pl
from jax.experimental.pallas import tpu as pltpu
from jax.sharding import Mesh, PartitionSpec as P

sharpness_multiplier = 10.0
sigmoid_shift_constant = -2.0
loss_scale = 32.0
epsilon = 1e-06
DP = ("z", "xl", "y")
MP = ("xh", "c")
NEAR = ("xl", "y")
ROWS, WIDTH, SHARD = 384, 1152, 288
WHOLE, REST, PACKED = 256, 32, 432
BF, F32 = jnp.bfloat16, jnp.float32


def swapped(block, axis, bit):
    return lax.ppermute(block, axis, [(i, i ^ bit) for i in range(lax.axis_size(axis))])


def gathered(block, other_x):
    across = other_x(block)
    return [block, across, swapped(block, "c", 1), swapped(across, "c", 1)]


def packed(embed):
    rest = embed[:, WHOLE:].reshape(8, ROWS // 8, REST).transpose(1, 0, 2)
    return jnp.concatenate([embed[:, :WHOLE], rest.reshape(ROWS // 8, WHOLE)])


def nn(a, b):
    return jnp.dot(a, b, preferred_element_type=F32)


def nt(a, b):
    return lax.dot_general(a, b, (((1,), (1,)), ((), ())), preferred_element_type=F32)


def unpacked_rest(blocks, t):
    group = ROWS // 8
    lane = lax.broadcasted_iota(jnp.int32, (group, 128), 1) // REST
    pieces = []
    for i in range(8):
        at = i // 4 * 128
        total = jnp.zeros((group, 128), F32)
        for b, block in enumerate(blocks):
            part = block[t, ROWS:, at : at + 128].astype(F32)
            shift = (b - i) % 4 * REST
            if shift:
                part = pltpu.roll(part, shift, axis=1)
            total = jnp.where(lane == b, part, total)
        pieces.append(total.astype(BF))
    return jnp.concatenate(pieces, axis=0)


def project(heads, blocks, t, hid):
    rest = unpacked_rest(blocks, t)

    @pl.loop(0, 3)
    def _(n):
        cols = pl.ds(pl.multiple_of(n * 384, 384), 384)
        total = nn(rest, jnp.concatenate([h[t, WHOLE:, cols] for h in heads], axis=0))
        for h, e in zip(heads, blocks):
            total += nn(e[t, :ROWS, :], h[t, :WHOLE, cols])
        hid[:, cols] = total


def norm_of(hid):
    return jnp.sqrt(jnp.sum(hid[...] * hid[...], axis=1, keepdims=True) + epsilon)


def grads_of(dots, same):
    z = sharpness_multiplier * dots + sigmoid_shift_constant
    s = 1.0 / (1.0 + jnp.exp(jnp.where(same, z, -z)))
    return (jnp.where(same, -loss_scale, loss_scale) * s).astype(BF)


def near_kernel(*refs):
    heads, own, far = refs[0:4], refs[4:8], refs[8:12]
    img_embed, txt_embed, col_ids, row_ids = refs[12:16]
    hid_i, hid_t, unit_i, unit_t, d_i, d_t, norm_i, norm_t, xt_i, xt_t = refs[16:26]
    hid, unit = refs[26:]
    for t, (h, u, n) in enumerate(((hid_i, unit_i, norm_i), (hid_t, unit_t, norm_t))):
        project(heads, own, t, h)
        n[...] = norm_of(h)
        u[...] = (h[...] / n[...]).astype(BF)
    g = grads_of(nt(unit_i[...], unit_t[...]), col_ids[...] == row_ids[0:1, :])
    d_i[...] = nn(g, unit_t[...])
    d_t[...] = nn(g.T, unit_i[...])
    same = col_ids[...] == row_ids[2:3, :]
    for t, (mine, d) in enumerate(((unit_t, d_t), (unit_i, d_i))):
        project(heads, far, t, hid)
        unit[...] = (hid[...] / norm_of(hid)).astype(BF)
        g = grads_of(nt(mine[...], unit[...]), same)
        d[...] += nn(g, unit[...])
    xt_i[...] = img_embed[...].T
    xt_t[...] = txt_embed[...].T


def far_kernel(*refs):
    heads, far = refs[0:4], refs[4:8]
    hid_i, hid_t, unit_i, unit_t, d_i, d_t, norm_i, norm_t, xt_i, xt_t = refs[8:18]
    col_ids, row_ids, grad_i, grad_t, w, hid, unit = refs[18:]
    same = col_ids[...] == row_ids[1:2, :]
    order = (
        (1, unit_i, d_i, hid_i, norm_i, xt_i, grad_i, 0),
        (0, unit_t, d_t, hid_t, norm_t, xt_t, grad_t, 1),
    )
    for t, mine, d, h, n, xt, grad, out in order:
        project(heads, far, t, hid)
        unit[...] = (hid[...] / norm_of(hid)).astype(BF)
        g = grads_of(nt(mine[...], unit[...]), same)
        full = sharpness_multiplier * (d[...] + nn(g, unit[...]))
        norm = n[...]
        along = jnp.sum(h[...] * full, axis=1, keepdims=True) / (norm * norm * norm)
        dhid = (full / norm - h[...] * along).astype(BF)
        w[out * SHARD : (out + 1) * SHARD, :] = nn(xt[...], dhid).astype(BF)
        grad[...] = nt(dhid, heads[0][out]).astype(BF)


def call(kernel, out, scratch, flops, args):
    out = [jax.ShapeDtypeStruct(s, d) for s, d in out]
    size = sum(a.size * a.dtype.itemsize for a in args) + sum(o.size * o.dtype.itemsize for o in out)
    return pl.pallas_call(
        kernel,
        out_shape=out,
        in_specs=[pl.BlockSpec(memory_space=pltpu.VMEM)] * len(args),
        out_specs=[pl.BlockSpec(memory_space=pltpu.VMEM)] * len(out),
        scratch_shapes=scratch,
        compiler_params=pltpu.CompilerParams(vmem_limit_bytes=40 << 20),
        cost_estimate=pl.CostEstimate(flops=flops, bytes_accessed=size, transcendentals=ROWS * WIDTH),
    )(*args)


def summed_over_dp(both):
    rows, width = both.shape
    near = lax.axis_size("xl") * lax.axis_size("y")
    far = lax.axis_size("z")
    share = rows // near
    parts = lax.all_to_all(both.reshape(near, share, width), NEAR, 0, 0, tiled=True)
    part = jnp.sum(parts.astype(F32), axis=0)
    tr, tc = share // 8, width // 128
    tiles = part.reshape(tr, 8, tc, 128).transpose(0, 2, 1, 3).reshape(tr * tc, 8, 128)
    each = -(-tr * tc // far)
    tiles = jnp.pad(tiles, ((0, each * far - tr * tc), (0, 0), (0, 0))).astype(BF)
    pieces = lax.all_to_all(tiles.reshape(far, each * 8, 128), "z", 0, 0, tiled=True)
    piece = jnp.sum(pieces.astype(F32), axis=0).astype(BF)
    full = lax.all_gather(piece, "z", axis=0)
    full = full.reshape(each * far, 8, 128)[: tr * tc]
    full = full.reshape(tr, tc, 8, 128).transpose(0, 2, 1, 3).reshape(share, width)
    everyone = lax.all_to_all(
        jnp.broadcast_to(full[None], (near, share, width)), NEAR, 0, 0, tiled=True
    )
    return everyone.reshape(rows, width).astype(F32)


def body(img_embed, txt_embed, img_head, txt_head, pair_ids):
    groups = lax.axis_size(DP)
    me = lax.axis_index(DP)
    own = jnp.stack([packed(img_embed), packed(txt_embed)])
    heads = jnp.stack([img_head, txt_head])

    def across(block):
        return swapped(block, "xh", 1)

    def adjacent(block):
        return lax.ppermute(block, ("xl", "xh"), [(i, i ^ 3) for i in range(4)])

    far_z = swapped(own, "z", lax.axis_size("z") // 2)
    far_y = swapped(own, "y", 1)
    heads4 = gathered(heads, adjacent)
    own4 = gathered(own, across)
    far_y4 = gathered(far_y, across)
    far_z4 = gathered(far_z, across)
    table = pair_ids.reshape(groups, ROWS)
    places = [me, jnp.bitwise_xor(me, groups // 2), jnp.bitwise_xor(me, 1)]
    row_ids = jnp.concatenate([lax.dynamic_slice_in_dim(table, p, 1) for p in places])
    col_ids = row_ids[0][:, None]

    big, half = ((ROWS, WIDTH), F32), ((ROWS, WIDTH), BF)
    scratch = [pltpu.VMEM(*big), pltpu.VMEM(*half)]
    unit_flops = 2 * ROWS * WIDTH
    state = call(
        near_kernel,
        [big, big, half, half, big, big] + [((ROWS, 1), F32)] * 2 + [((SHARD, ROWS), BF)] * 2,
        scratch,
        unit_flops * (4 * WIDTH + 7 * ROWS),
        heads4 + own4 + far_y4 + [img_embed, txt_embed, col_ids, row_ids],
    )
    img_grad, txt_grad, w = call(
        far_kernel,
        [((ROWS, SHARD), BF)] * 2 + [((2 * SHARD, WIDTH), BF)],
        scratch,
        unit_flops * (2 * WIDTH + 4 * ROWS + 4 * SHARD),
        heads4 + far_z4 + list(state) + [col_ids, row_ids],
    )
    w = summed_over_dp(w) * (1.0 / jnp.sqrt(jnp.float32(groups * ROWS)))
    return img_grad, txt_grad, w[:SHARD], w[SHARD:]


def solution(mesh):
    fine = Mesh(mesh.devices.reshape(16, 2, 4, 2, 2), DP + MP)
    return jax.shard_map(
        body,
        mesh=fine,
        in_specs=(P(DP, MP), P(DP, MP), P(MP, None), P(MP, None), P()),
        out_specs=(P(DP, MP), P(DP, MP), P(MP, None), P(MP, None)),
        check_vma=False,
    )
```

```python
import jax
import jax.numpy as jnp
from jax import lax
from jax.experimental import pallas as pl
from jax.experimental.pallas import tpu as pltpu
from jax.sharding import Mesh, PartitionSpec as P

sharpness_multiplier = 10.0
sigmoid_shift_constant = -2.0
loss_scale = 32.0
epsilon = 1e-06
DP = ("z", "xl", "y")
MP = ("xh", "c")
NEAR = ("xl", "y")
ROWS, WIDTH, SHARD = 384, 1152, 288
BF, F32 = jnp.bfloat16, jnp.float32


def swapped(block, axis, bit):
    return lax.ppermute(block, axis, [(i, i ^ bit) for i in range(lax.axis_size(axis))])


def nn(a, b):
    return jnp.dot(a, b, preferred_element_type=F32)


def nt(a, b):
    return lax.dot_general(a, b, (((1,), (1,)), ((), ())), preferred_element_type=F32)


def joined(blocks, t):
    return jnp.concatenate([b[t] for b in blocks], axis=0)


def project(head, blocks, t, hid):
    hid[...] = nn(head[t], joined(blocks, t))


def norm_of(hid):
    return jnp.sqrt(jnp.sum(hid[...] * hid[...], axis=0, keepdims=True) + epsilon)


def grads_of(dots, same):
    z = sharpness_multiplier * dots + sigmoid_shift_constant
    s = 1.0 / (1.0 + jnp.exp(jnp.where(same, z, -z)))
    return (jnp.where(same, -loss_scale, loss_scale) * s).astype(BF)


def near_kernel(*refs):
    heads, own, far = refs[0:4], refs[4:8], refs[8:12]
    col_ids, row_ids = refs[12:14]
    turned, hid_i, hid_t, rows_i, rows_t, d_i, d_t, norm_i, norm_t = refs[14:23]
    hid, unit_i, unit_t = refs[23:]
    for t, (h, u, r, n) in enumerate(((hid_i, unit_i, rows_i, norm_i), (hid_t, unit_t, rows_t, norm_t))):
        turned[t] = joined(heads, t).T
        project(turned, own, t, h)
        n[...] = norm_of(h)
        u[...] = (h[...] / n[...]).astype(BF)
        r[...] = u[...].T
    g = grads_of(nn(rows_i[...], unit_t[...]), col_ids[...] == row_ids[0:1, :])
    d_i[...] = nt(unit_t[...], g)
    d_t[...] = nn(unit_i[...], g)
    same = col_ids[...] == row_ids[2:3, :]
    for t, (rows, unit, d) in enumerate(((rows_t, unit_t, d_t), (rows_i, unit_i, d_i))):
        project(turned, far, t, hid)
        unit[...] = (hid[...] / norm_of(hid)).astype(BF)
        g = grads_of(nn(rows[...], unit[...]), same)
        d[...] += nt(unit[...], g)


def far_kernel(*refs):
    heads, far, img_embed, txt_embed, col_ids, row_ids = refs[0], refs[1:5], *refs[5:9]
    turned, hid_i, hid_t, rows_i, rows_t, d_i, d_t, norm_i, norm_t = refs[9:18]
    grad_i, grad_t, w, hid, unit = refs[18:]
    same = col_ids[...] == row_ids[1:2, :]
    order = (
        (1, rows_i, d_i, hid_i, norm_i, img_embed, grad_i, 0),
        (0, rows_t, d_t, hid_t, norm_t, txt_embed, grad_t, 1),
    )
    for t, rows, d, h, n, embed, grad, out in order:
        project(turned, far, t, hid)
        unit[...] = (hid[...] / norm_of(hid)).astype(BF)
        g = grads_of(nn(rows[...], unit[...]), same)
        full = sharpness_multiplier * (d[...] + nt(unit[...], g))
        norm = n[...]
        along = jnp.sum(h[...] * full, axis=0, keepdims=True) / (norm * norm * norm)
        dhid = (full / norm - h[...] * along).astype(BF)
        w[out * SHARD : (out + 1) * SHARD, :] = nt(embed[...], dhid).astype(BF)
        grad[...] = nn(heads[out], dhid).astype(BF)


def call(kernel, out, scratch, flops, args):
    out = [jax.ShapeDtypeStruct(s, d) for s, d in out]
    size = sum(a.size * a.dtype.itemsize for a in args) + sum(o.size * o.dtype.itemsize for o in out)
    return pl.pallas_call(
        kernel,
        out_shape=out,
        in_specs=[pl.BlockSpec(memory_space=pltpu.VMEM)] * len(args),
        out_specs=[pl.BlockSpec(memory_space=pltpu.VMEM)] * len(out),
        scratch_shapes=scratch,
        compiler_params=pltpu.CompilerParams(vmem_limit_bytes=40 << 20),
        cost_estimate=pl.CostEstimate(flops=flops, bytes_accessed=size, transcendentals=ROWS * WIDTH),
    )(*args)


def summed_over_dp(both):
    rows, width = both.shape
    near = lax.axis_size("xl") * lax.axis_size("y")
    far = lax.axis_size("z")
    share = rows // near
    parts = lax.all_to_all(both.reshape(near, share, width), NEAR, 0, 0, tiled=True)
    part = jnp.sum(parts.astype(F32), axis=0)
    tr, tc = share // 8, width // 128
    tiles = part.reshape(tr, 8, tc, 128).transpose(0, 2, 1, 3).reshape(tr * tc, 8, 128)
    each = -(-tr * tc // far)
    tiles = jnp.pad(tiles, ((0, each * far - tr * tc), (0, 0), (0, 0))).astype(BF)
    pieces = lax.all_to_all(tiles.reshape(far, each * 8, 128), "z", 0, 0, tiled=True)
    piece = jnp.sum(pieces.astype(F32), axis=0).astype(BF)
    full = lax.all_gather(piece, "z", axis=0)
    full = full.reshape(each * far, 8, 128)[: tr * tc]
    full = full.reshape(tr, tc, 8, 128).transpose(0, 2, 1, 3).reshape(share, width)
    everyone = lax.all_to_all(
        jnp.broadcast_to(full[None], (near, share, width)), NEAR, 0, 0, tiled=True
    )
    return everyone.reshape(rows, width).astype(F32)


def body(img_embed, txt_embed, img_head, txt_head, pair_ids):
    groups = lax.axis_size(DP)
    me = lax.axis_index(DP)
    img_t, txt_t = img_embed.T, txt_embed.T

    def across(block):
        return swapped(block, "xh", 1)

    def adjacent(block):
        return lax.ppermute(block, ("xl", "xh"), [(i, i ^ 3) for i in range(4)])

    own = jnp.stack([img_t, txt_t])
    heads = jnp.stack([img_head, txt_head])
    far_z = swapped(own, "z", lax.axis_size("z") // 2)
    heads_x, own_x, far_y = adjacent(heads), across(own), swapped(own, "y", 1)
    far_y_x = lax.ppermute(own, ("y", "xh"), [(i, i ^ 3) for i in range(2 * lax.axis_size("y"))])
    far_z, far_y_x, own, own_x, far_y = lax.optimization_barrier((far_z, far_y_x, own, own_x, far_y))
    heads4 = [heads, heads_x, swapped(heads, "c", 1), swapped(heads_x, "c", 1)]
    own4 = [own, own_x, swapped(own, "c", 1), swapped(own_x, "c", 1)]
    far_y4 = [far_y, far_y_x, swapped(far_y, "c", 1), swapped(far_y_x, "c", 1)]
    far_x = across(far_z)
    far_c = swapped(far_z, "c", 1)
    table = pair_ids.reshape(groups, ROWS)
    places = [me, jnp.bitwise_xor(me, groups // 2), jnp.bitwise_xor(me, 1)]
    row_ids = jnp.concatenate([lax.dynamic_slice_in_dim(table, p, 1) for p in places])
    col_ids = row_ids[0][:, None]

    big, half, line = ((WIDTH, ROWS), F32), ((WIDTH, ROWS), BF), ((1, ROWS), F32)
    rows = ((ROWS, WIDTH), BF)
    unit_flops = 2 * ROWS * WIDTH
    state = call(
        near_kernel,
        [((2, WIDTH, WIDTH), BF), big, big, rows, rows, big, big, line, line],
        [pltpu.VMEM(*s) for s in (big, half, half)],
        unit_flops,
        heads4 + own4 + far_y4 + [col_ids, row_ids],
    )
    state, far_x = lax.optimization_barrier((state, far_x))
    far_z4 = [far_z, far_x, far_c, swapped(far_x, "c", 1)]
    img_grad, txt_grad, w = call(
        far_kernel,
        [((SHARD, ROWS), BF)] * 2 + [((2 * SHARD, WIDTH), BF)],
        [pltpu.VMEM(*s) for s in (big, half)],
        3 * unit_flops * (2 * WIDTH + 4 * ROWS + 4 * SHARD),
        [heads] + far_z4 + [img_t, txt_t, col_ids, row_ids] + list(state),
    )
    w = summed_over_dp(w) * (1.0 / jnp.sqrt(jnp.float32(groups * ROWS)))
    return img_grad.T, txt_grad.T, w[:SHARD], w[SHARD:]


def solution(mesh):
    fine = Mesh(mesh.devices.reshape(16, 2, 4, 2, 2), DP + MP)
    return jax.shard_map(
        body,
        mesh=fine,
        in_specs=(P(DP, MP), P(DP, MP), P(MP, None), P(MP, None), P()),
        out_specs=(P(DP, MP), P(DP, MP), P(MP, None), P(MP, None)),
        check_vma=False,
    )
```

```python
import functools

import jax
import jax.numpy as jnp
import numpy as np
from jax import lax
from jax.experimental import pallas as pl
from jax.experimental.pallas import tpu as pltpu
from jax.sharding import Mesh, PartitionSpec as P

sharpness_multiplier = 10.0
sigmoid_shift_constant = -2.0
loss_scale = 32.0
epsilon = 1e-06
DP = ("z", "xl", "y")
MP = ("xh", "c")
NEAR = ("xl", "y")
ROWS, WIDTH, SHARD, LANES = 384, 1152, 288, 128
SPREAD = 2688
BF, F32 = jnp.bfloat16, jnp.float32


def swapped(block, axis, bit):
    return lax.ppermute(block, axis, [(i, i ^ bit) for i in range(lax.axis_size(axis))])


def nn(a, b):
    return jnp.dot(a, b, preferred_element_type=F32)


def nt(a, b):
    return lax.dot_general(a, b, (((1,), (1,)), ((), ())), preferred_element_type=F32)


def joined(blocks, t):
    return jnp.concatenate([b[t] for b in blocks], axis=0)


def project(head, blocks, t, hid):
    hid[...] = nn(head[t], joined(blocks, t))


def norm_of(hid):
    return jnp.sqrt(jnp.sum(hid[...] * hid[...], axis=0, keepdims=True) + epsilon)


def grads_of(dots, same):
    z = sharpness_multiplier * dots + sigmoid_shift_constant
    s = 1.0 / (1.0 + jnp.exp(jnp.where(same, z, -z)))
    return (jnp.where(same, -loss_scale, loss_scale) * s).astype(BF)


def near_kernel(*refs):
    both, both_c, near, near_c, col_ids, row_ids = refs[0:6]
    turned, hid_i, hid_t, rows_i, rows_t, d_i, d_t, norm_i, norm_t = refs[6:15]
    hid, unit_i, unit_t = refs[15:]
    heads = [r.at[k] for r in (both, both_c) for k in (0, 1)]
    own = [r.at[k] for r in (near, near_c) for k in (0, 1)]
    far = [r.at[k] for r in (near, near_c) for k in (2, 3)]
    for t, (h, u, r, n) in enumerate(((hid_i, unit_i, rows_i, norm_i), (hid_t, unit_t, rows_t, norm_t))):
        turned[t] = joined(heads, t).T
        project(turned, own, t, h)
        n[...] = norm_of(h)
        u[...] = (h[...] / n[...]).astype(BF)
        r[...] = u[...].T
    g = grads_of(nn(rows_i[...], unit_t[...]), col_ids[...] == row_ids[0:1, :])
    d_i[...] = nt(unit_t[...], g)
    d_t[...] = nn(unit_i[...], g)
    same = col_ids[...] == row_ids[2:3, :]
    for t, (rows, unit, d) in enumerate(((rows_t, unit_t, d_t), (rows_i, unit_i, d_i))):
        project(turned, far, t, hid)
        unit[...] = (hid[...] / norm_of(hid)).astype(BF)
        g = grads_of(nn(rows[...], unit[...]), same)
        d[...] += nt(unit[...], g)


def far_kernel(tower, *refs):
    heads, far, embed, col_ids, row_ids = refs[0], refs[1:5], *refs[5:8]
    turned, h, rows, d, n = refs[8:13]
    grad, w, hid, unit = refs[13:]
    project(turned, far, 1 - tower, hid)
    unit[...] = (hid[...] / norm_of(hid)).astype(BF)
    g = grads_of(nn(rows[...], unit[...]), col_ids[...] == row_ids[1:2, :])
    full = sharpness_multiplier * (d[...] + nt(unit[...], g))
    norm = n[...]
    along = jnp.sum(h[...] * full, axis=0, keepdims=True) / (norm * norm * norm)
    dhid = (full / norm - h[...] * along).astype(BF)
    total = nt(embed[...], dhid).astype(BF)
    for k in range(WIDTH // LANES):
        w[k * SHARD : (k + 1) * SHARD, :] = total[:, k * LANES : (k + 1) * LANES]
    w[WIDTH // LANES * SHARD :, :] = jnp.zeros((SPREAD - WIDTH // LANES * SHARD, LANES), BF)
    grad[...] = nn(heads[tower], dhid).astype(BF)


def call(kernel, out, scratch, flops, args):
    out = [jax.ShapeDtypeStruct(s, d) for s, d in out]
    size = sum(a.size * a.dtype.itemsize for a in args) + sum(o.size * o.dtype.itemsize for o in out)
    return pl.pallas_call(
        kernel,
        out_shape=out,
        in_specs=[pl.BlockSpec(memory_space=pltpu.VMEM)] * len(args),
        out_specs=[pl.BlockSpec(memory_space=pltpu.VMEM)] * len(out),
        scratch_shapes=scratch,
        compiler_params=pltpu.CompilerParams(vmem_limit_bytes=24 << 20),
        cost_estimate=pl.CostEstimate(flops=flops, bytes_accessed=size, transcendentals=ROWS * WIDTH),
    )(*args)


def scattered(w):
    near = lax.axis_size("xl") * lax.axis_size("y")
    parts = lax.all_to_all(w.reshape(near, SPREAD // near, LANES), NEAR, 0, 0, tiled=True)
    return jnp.sum(parts.astype(F32), axis=0)


def summed_over_z(part):
    count, rows = lax.axis_size("z"), part.shape[0]
    each = -(-rows // (count * 8)) * 8
    padded = jnp.pad(part, ((0, each * count - rows), (0, 0))).astype(BF)
    pieces = lax.all_to_all(padded.reshape(count, each, LANES), "z", 0, 0, tiled=True)
    piece = jnp.sum(pieces.astype(F32), axis=0).astype(BF)
    return lax.all_gather(piece, "z", axis=0, tiled=True)[:rows]


def everywhere(part):
    near = lax.axis_size("xl") * lax.axis_size("y")
    return lax.all_to_all(jnp.broadcast_to(part[None], (near, *part.shape)), NEAR, 0, 0, tiled=True)


def unspread_kernel(factor, w, img, txt):
    piece = SPREAD // w.shape[0]
    for t, out in enumerate((img, txt)):
        for k in range(WIDTH // LANES):
            row = k * SHARD
            while row < (k + 1) * SHARD:
                at, inside = divmod(row, piece)
                size = min(piece - inside, (k + 1) * SHARD - row)
                start = t * piece + inside
                out[row - k * SHARD : row - k * SHARD + size, k * LANES : (k + 1) * LANES] = (
                    w[at, start : start + size, :].astype(F32) * factor
                )
                row += size


def body(img_embed, txt_embed, img_head, txt_head, pair_ids):
    groups = lax.axis_size(DP)
    me = lax.axis_index(DP)
    img_t, txt_t = img_embed.T, txt_embed.T

    def across(block):
        return swapped(block, "xh", 1)

    def adjacent(block):
        return lax.ppermute(block, ("xl", "xh"), [(i, i ^ 3) for i in range(4)])

    own = jnp.stack([img_t, txt_t])
    heads = jnp.stack([img_head, txt_head])
    far_z = swapped(own, "z", lax.axis_size("z") // 2)
    heads_x, own_x, far_y = adjacent(heads), across(own), swapped(own, "y", 1)
    far_y_x = lax.ppermute(own, ("y", "xh"), [(i, i ^ 3) for i in range(2 * lax.axis_size("y"))])
    table = pair_ids.reshape(groups, ROWS)
    places = [me, jnp.bitwise_xor(me, groups // 2), jnp.bitwise_xor(me, 1)]
    row_ids = jnp.concatenate([lax.dynamic_slice_in_dim(table, p, 1) for p in places])
    col_ids = row_ids[0][:, None]
    far_z, far_y_x, own_x, far_y, heads_x, row_ids, col_ids = lax.optimization_barrier(
        (far_z, far_y_x, own_x, far_y, heads_x, row_ids, col_ids)
    )
    near = jnp.stack([own, own_x, far_y, far_y_x])
    near_c = swapped(near, "c", 1)
    both = jnp.stack([heads, heads_x])
    both_c = swapped(both, "c", 1)
    far_x = across(far_z)
    far_c = swapped(far_z, "c", 1)

    big, half, line = ((WIDTH, ROWS), F32), ((WIDTH, ROWS), BF), ((1, ROWS), F32)
    rows = ((ROWS, WIDTH), BF)
    unit_flops = 2 * ROWS * WIDTH
    state = call(
        near_kernel,
        [((2, WIDTH, WIDTH), BF), big, big, rows, rows, big, big, line, line],
        [pltpu.VMEM(*s) for s in (big, half, half)],
        unit_flops,
        [both, both_c, near, near_c, col_ids, row_ids],
    )
    state, far_x = lax.optimization_barrier((state, far_x))
    far_z4 = [far_z, far_x, far_c, swapped(far_x, "c", 1)]
    turned, hid_i, hid_t, rows_i, rows_t, d_i, d_t, norm_i, norm_t = state

    def far(tower, embed, *rest):
        return call(
            functools.partial(far_kernel, tower),
            [((SHARD, ROWS), BF), ((SPREAD, LANES), BF)],
            [pltpu.VMEM(*s) for s in (big, half)],
            3 * ROWS * WIDTH * (2 * WIDTH + 4 * ROWS + 4 * SHARD),
            [heads] + far_z4 + [embed, col_ids, row_ids, turned, *rest],
        )

    img_grad, img_w = far(0, img_t, hid_i, rows_i, d_i, norm_i)
    txt_grad, txt_w = far(1, txt_t, hid_t, rows_t, d_t, norm_t)
    part = jnp.concatenate([scattered(img_w), scattered(txt_w)])
    w = everywhere(summed_over_z(part))
    factor = float(1.0 / np.sqrt(np.float32(groups * ROWS)))
    img_w, txt_w = pl.pallas_call(
        functools.partial(unspread_kernel, factor),
        out_shape=[jax.ShapeDtypeStruct((SHARD, WIDTH), F32)] * 2,
        compiler_params=pltpu.CompilerParams(vmem_limit_bytes=24 << 20),
    )(w)
    return img_grad.T, txt_grad.T, img_w, txt_w


def solution(mesh):
    fine = Mesh(mesh.devices.reshape(16, 2, 4, 2, 2), DP + MP)
    return jax.shard_map(
        body,
        mesh=fine,
        in_specs=(P(DP, MP), P(DP, MP), P(MP, None), P(MP, None), P()),
        out_specs=(P(DP, MP), P(DP, MP), P(MP, None), P(MP, None)),
        check_vma=False,
    )
```

```python
import functools

import jax
import jax.numpy as jnp
import numpy as np
from jax import lax
from jax.experimental import pallas as pl
from jax.experimental.pallas import tpu as pltpu
from jax.sharding import Mesh, PartitionSpec as P

sharpness_multiplier = 10.0
sigmoid_shift_constant = -2.0
loss_scale = 32.0
epsilon = 1e-06
DP = ("z", "xl", "y")
MP = ("xh", "c")
NEAR = ("xl", "y")
ROWS, WIDTH, SHARD, LANES = 384, 1152, 288, 128
EIGHTHS = 8
SPREAD = 2688
BF, F32 = jnp.bfloat16, jnp.float32


def swapped(block, axis, bit):
    return lax.ppermute(block, axis, [(i, i ^ bit) for i in range(lax.axis_size(axis))])


def nn(a, b):
    return jnp.dot(a, b, preferred_element_type=F32)


def nt(a, b):
    return lax.dot_general(a, b, (((1,), (1,)), ((), ())), preferred_element_type=F32)


def joined(blocks, t):
    return jnp.concatenate([b[t] for b in blocks], axis=0)


def project(head, blocks, t, hid):
    hid[...] = nn(head[t], joined(blocks, t))


def norm_of(hid):
    return jnp.sqrt(jnp.sum(hid[...] * hid[...], axis=0, keepdims=True) + epsilon)


def grads_of(dots, same):
    z = sharpness_multiplier * dots + sigmoid_shift_constant
    s = 1.0 / (1.0 + jnp.exp(jnp.where(same, z, -z)))
    return (jnp.where(same, -loss_scale, loss_scale) * s).astype(BF)


def near_kernel(*refs):
    heads, (near, near_c, col_ids, row_ids) = refs[0:4], refs[4:8]
    turned, hid_i, hid_t, rows_i, rows_t, d_i, d_t, inv_i, inv_t = refs[8:17]
    hid, unit_i, unit_t = refs[17:]
    own = [r.at[k] for r in (near, near_c) for k in (0, 1)]
    far = [r.at[k] for r in (near, near_c) for k in (2, 3)]
    for t, (h, u, r, n) in enumerate(((hid_i, unit_i, rows_i, inv_i), (hid_t, unit_t, rows_t, inv_t))):
        turned[t] = joined(heads, t).T
        project(turned, own, t, h)
        n[...] = 1.0 / norm_of(h)
        u[...] = (h[...] * n[...]).astype(BF)
        r[...] = u[...].T
    g = grads_of(nn(rows_i[...], unit_t[...]), col_ids[...] == row_ids[0:1, :])
    d_i[...] = nt(unit_t[...], g)
    d_t[...] = nn(unit_i[...], g)
    same = col_ids[...] == row_ids[2:3, :]
    for t, (rows, unit, d) in enumerate(((rows_t, unit_t, d_t), (rows_i, unit_i, d_i))):
        project(turned, far, t, hid)
        unit[...] = (hid[...] * (1.0 / norm_of(hid))).astype(BF)
        g = grads_of(nn(rows[...], unit[...]), same)
        d[...] += nt(unit[...], g)


def cut(tower, block):
    piece, row, stop = SPREAD // EIGHTHS, block * SHARD, (block + 1) * SHARD
    while row < stop:
        eighth, inside = divmod(row, piece)
        count = min(piece - inside, stop - row)
        yield row - block * SHARD, count, eighth, tower * piece + inside
        row += count


def far_kernel(*refs):
    heads, far, img_embed, txt_embed, col_ids, row_ids = refs[0], refs[1:5], *refs[5:9]
    turned, hid_i, hid_t, rows_i, rows_t, d_i, d_t, inv_i, inv_t = refs[9:18]
    grad_i, grad_t, w, hid, unit = refs[18:]
    same = col_ids[...] == row_ids[1:2, :]
    order = (
        (0, rows_i, d_i, hid_i, inv_i, img_embed, grad_i),
        (1, rows_t, d_t, hid_t, inv_t, txt_embed, grad_t),
    )
    for tower, rows, d, h, n, embed, grad in order:
        project(turned, far, 1 - tower, hid)
        unit[...] = (hid[...] * (1.0 / norm_of(hid))).astype(BF)
        g = grads_of(nn(rows[...], unit[...]), same)
        full = sharpness_multiplier * (d[...] + nt(unit[...], g))
        scale = n[...]
        along = jnp.sum(h[...] * full, axis=0, keepdims=True) * (scale * scale)
        dhid = ((full - h[...] * along) * scale).astype(BF)
        total = nt(embed[...], dhid).astype(BF)
        for k in range(WIDTH // LANES):
            for row, count, eighth, at in cut(tower, k):
                w[eighth, at : at + count, :] = total[row : row + count, k * LANES : (k + 1) * LANES]
        piece = SPREAD // EIGHTHS
        used = WIDTH // LANES * SHARD - (EIGHTHS - 1) * piece
        w[EIGHTHS - 1, tower * piece + used : (tower + 1) * piece, :] = jnp.zeros((piece - used, LANES), BF)
        grad[...] = nn(heads[tower], dhid).astype(BF)


def call(kernel, out, scratch, flops, args):
    out = [jax.ShapeDtypeStruct(s, d) for s, d in out]
    size = sum(a.size * a.dtype.itemsize for a in args) + sum(o.size * o.dtype.itemsize for o in out)
    return pl.pallas_call(
        kernel,
        out_shape=out,
        in_specs=[pl.BlockSpec(memory_space=pltpu.VMEM)] * len(args),
        out_specs=[pl.BlockSpec(memory_space=pltpu.VMEM)] * len(out),
        scratch_shapes=scratch,
        compiler_params=pltpu.CompilerParams(vmem_limit_bytes=24 << 20),
        cost_estimate=pl.CostEstimate(flops=flops, bytes_accessed=size, transcendentals=ROWS * WIDTH),
    )(*args)


def scattered(w):
    parts = lax.all_to_all(w, NEAR, 0, 0, tiled=True)
    return jnp.sum(parts.astype(F32), axis=0)


def summed_over_z(part):
    count, rows = lax.axis_size("z"), part.shape[0]
    each = -(-rows // (count * 8)) * 8
    padded = jnp.pad(part, ((0, each * count - rows), (0, 0))).astype(BF)
    pieces = lax.all_to_all(padded.reshape(count, each, LANES), "z", 0, 0, tiled=True)
    piece = jnp.sum(pieces.astype(F32), axis=0).astype(BF)
    return lax.all_gather(piece, "z", axis=0, tiled=True)[:rows]


def everywhere(part):
    return lax.all_to_all(jnp.broadcast_to(part[None], (EIGHTHS, *part.shape)), NEAR, 0, 0, tiled=True)


def unspread_kernel(factor, w, img, txt):
    for t, out in enumerate((img, txt)):
        for k in range(WIDTH // LANES):
            for row, count, eighth, at in cut(t, k):
                out[row : row + count, k * LANES : (k + 1) * LANES] = (
                    w[eighth, at : at + count, :].astype(F32) * factor
                )


def body(img_embed, txt_embed, img_head, txt_head, pair_ids):
    groups = lax.axis_size(DP)
    me = lax.axis_index(DP)
    img_t, txt_t = img_embed.T, txt_embed.T

    def across(block):
        return swapped(block, "xh", 1)

    def adjacent(block):
        return lax.ppermute(block, ("xl", "xh"), [(i, i ^ 3) for i in range(4)])

    own = jnp.stack([img_t, txt_t])
    heads = jnp.stack([img_head, txt_head])
    far_z = swapped(own, "z", lax.axis_size("z") // 2)
    heads_x, own_x, far_y = adjacent(heads), across(own), swapped(own, "y", 1)
    far_y_x = lax.ppermute(own, ("y", "xh"), [(i, i ^ 3) for i in range(2 * lax.axis_size("y"))])
    table = pair_ids.reshape(groups, ROWS)
    places = [me, jnp.bitwise_xor(me, groups // 2), jnp.bitwise_xor(me, 1)]
    row_ids = jnp.concatenate([lax.dynamic_slice_in_dim(table, p, 1) for p in places])
    col_ids = row_ids[0][:, None]
    far_z, far_y_x, own_x, far_y, row_ids, col_ids = lax.optimization_barrier(
        (far_z, far_y_x, own_x, far_y, row_ids, col_ids)
    )
    near = jnp.stack([own, own_x, far_y, far_y_x])
    near_c = swapped(near, "c", 1)
    heads_c, heads_xc = swapped(heads, "c", 1), swapped(heads_x, "c", 1)
    far_x = across(far_z)
    far_c = swapped(far_z, "c", 1)

    big, half, line = ((WIDTH, ROWS), F32), ((WIDTH, ROWS), BF), ((1, ROWS), F32)
    rows = ((ROWS, WIDTH), BF)
    unit_flops = 2 * ROWS * WIDTH
    state = call(
        near_kernel,
        [((2, WIDTH, WIDTH), BF), big, big, rows, rows, big, big, line, line],
        [pltpu.VMEM(*s) for s in (big, half, half)],
        unit_flops,
        [heads, heads_x, heads_c, heads_xc, near, near_c, col_ids, row_ids],
    )
    state, far_x = lax.optimization_barrier((state, far_x))
    far_z4 = [far_z, far_x, far_c, swapped(far_x, "c", 1)]
    img_grad, txt_grad, w = call(
        far_kernel,
        [((SHARD, ROWS), BF)] * 2 + [((EIGHTHS, 2 * SPREAD // EIGHTHS, LANES), BF)],
        [pltpu.VMEM(*s) for s in (big, half)],
        3 * unit_flops * (2 * WIDTH + 4 * ROWS + 4 * SHARD),
        [heads] + far_z4 + [img_t, txt_t, col_ids, row_ids] + list(state),
    )
    w = everywhere(summed_over_z(scattered(w)))
    factor = float(1.0 / np.sqrt(np.float32(groups * ROWS)))
    img_w, txt_w = pl.pallas_call(
        functools.partial(unspread_kernel, factor),
        out_shape=[jax.ShapeDtypeStruct((SHARD, WIDTH), F32)] * 2,
        compiler_params=pltpu.CompilerParams(vmem_limit_bytes=24 << 20),
    )(w)
    return img_grad.T, txt_grad.T, img_w, txt_w


def solution(mesh):
    fine = Mesh(mesh.devices.reshape(16, 2, 4, 2, 2), DP + MP)
    return jax.shard_map(
        body,
        mesh=fine,
        in_specs=(P(DP, MP), P(DP, MP), P(MP, None), P(MP, None), P()),
        out_specs=(P(DP, MP), P(DP, MP), P(MP, None), P(MP, None)),
        check_vma=False,
    )
```

```python
import functools

import jax
import jax.numpy as jnp
import numpy as np
from jax import lax
from jax.experimental import pallas as pl
from jax.experimental.pallas import tpu as pltpu
from jax.sharding import Mesh, PartitionSpec as P

sharpness_multiplier = 10.0
sigmoid_shift_constant = -2.0
loss_scale = 32.0
epsilon = 1e-06
DP = ("zh", "zl", "xl", "y")
MP = ("xh", "c")
NEAR = ("zl", "xl", "y")
ROWS, WIDTH, SHARD, LANES = 384, 1152, 288, 128
PARTS = 16
SPREAD = 2816
BF, F32 = jnp.bfloat16, jnp.float32


def swapped(block, axis, bit):
    return lax.ppermute(block, axis, [(i, i ^ bit) for i in range(lax.axis_size(axis))])


def nn(a, b):
    return jnp.dot(a, b, preferred_element_type=F32)


def nt(a, b):
    return lax.dot_general(a, b, (((1,), (1,)), ((), ())), preferred_element_type=F32)


def joined(blocks, t):
    return jnp.concatenate([b[t] for b in blocks], axis=0)


def project(head, blocks, t, hid):
    hid[...] = nn(head[t], joined(blocks, t))


def norm_of(hid):
    return jnp.sqrt(jnp.sum(hid[...] * hid[...], axis=0, keepdims=True) + epsilon)


def grads_of(dots, same):
    z = sharpness_multiplier * dots + sigmoid_shift_constant
    s = 1.0 / (1.0 + jnp.exp(jnp.where(same, z, -z)))
    return (jnp.where(same, -loss_scale, loss_scale) * s).astype(BF)


def near_kernel(*refs):
    heads, (near, near_c, col_ids, row_ids) = refs[0:4], refs[4:8]
    turned, hid_i, hid_t, rows_i, rows_t, d_i, d_t, inv_i, inv_t = refs[8:17]
    hid, unit_i, unit_t = refs[17:]
    own = [r.at[k] for r in (near, near_c) for k in (0, 1)]
    far = [r.at[k] for r in (near, near_c) for k in (2, 3)]
    for t, (h, u, r, n) in enumerate(((hid_i, unit_i, rows_i, inv_i), (hid_t, unit_t, rows_t, inv_t))):
        turned[t] = joined(heads, t).T
        pair = nn(turned[t], jnp.concatenate([joined(own, t), joined(far, t)], axis=1))
        h[...] = pair[:, :ROWS]
        hid[t] = pair[:, ROWS:]
        n[...] = 1.0 / norm_of(h)
        u[...] = (h[...] * n[...]).astype(BF)
        r[...] = u[...].T
    g = grads_of(nn(rows_i[...], unit_t[...]), col_ids[...] == row_ids[0:1, :])
    d_i[...] = nt(unit_t[...], g)
    d_t[...] = nn(unit_i[...], g)
    same = col_ids[...] == row_ids[2:3, :]
    for t, (rows, unit, d) in enumerate(((rows_t, unit_t, d_t), (rows_i, unit_i, d_i))):
        unit[...] = (hid[t] * (1.0 / norm_of(hid.at[t]))).astype(BF)
        g = grads_of(nn(rows[...], unit[...]), same)
        d[...] += nt(unit[...], g)


def cut(tower, block, stop=0):
    piece, row = SPREAD // PARTS, block * SHARD
    stop = stop or row + SHARD
    while row < stop:
        part, inside = divmod(row, piece)
        count = min(piece - inside, stop - row)
        yield row - block * SHARD, count, part, tower * piece + inside
        row += count


def far_kernel(*refs):
    heads, far, img_embed, txt_embed, col_ids, row_ids = refs[0], refs[1:5], *refs[5:9]
    turned, hid_i, hid_t, rows_i, rows_t, d_i, d_t, inv_i, inv_t = refs[9:18]
    grad_i, grad_t, w, hid, unit = refs[18:]
    same = col_ids[...] == row_ids[1:2, :]
    order = (
        (0, rows_i, d_i, hid_i, inv_i, img_embed, grad_i),
        (1, rows_t, d_t, hid_t, inv_t, txt_embed, grad_t),
    )
    for tower, rows, d, h, n, embed, grad in order:
        project(turned, far, 1 - tower, hid)
        unit[...] = (hid[...] * (1.0 / norm_of(hid))).astype(BF)
        g = grads_of(nn(rows[...], unit[...]), same)
        full = sharpness_multiplier * (d[...] + nt(unit[...], g))
        scale = n[...]
        along = jnp.sum(h[...] * full, axis=0, keepdims=True) * (scale * scale)
        dhid = ((full - h[...] * along) * scale).astype(BF)
        total = nt(embed[...], dhid).astype(BF)
        for k in range(WIDTH // LANES):
            for row, count, part, at in cut(tower, k):
                w[part, at : at + count, :] = total[row : row + count, k * LANES : (k + 1) * LANES]
        for row, count, part, at in cut(tower, WIDTH // LANES, SPREAD):
            w[part, at : at + count, :] = jnp.zeros((count, LANES), BF)
        grad[...] = nn(heads[tower], dhid).astype(BF)


def call(kernel, out, scratch, flops, args):
    out = [jax.ShapeDtypeStruct(s, d) for s, d in out]
    size = sum(a.size * a.dtype.itemsize for a in args) + sum(o.size * o.dtype.itemsize for o in out)
    return pl.pallas_call(
        kernel,
        out_shape=out,
        in_specs=[pl.BlockSpec(memory_space=pltpu.VMEM)] * len(args),
        out_specs=[pl.BlockSpec(memory_space=pltpu.VMEM)] * len(out),
        scratch_shapes=scratch,
        compiler_params=pltpu.CompilerParams(vmem_limit_bytes=24 << 20),
        cost_estimate=pl.CostEstimate(flops=flops, bytes_accessed=size, transcendentals=ROWS * WIDTH),
    )(*args)


def scattered(w):
    parts = lax.all_to_all(w, NEAR, 0, 0, tiled=True)
    return jnp.sum(parts.astype(F32), axis=0)


def summed_over_far(part):
    count, rows = lax.axis_size("zh"), part.shape[0]
    each = -(-rows // (count * 8)) * 8
    padded = jnp.pad(part, ((0, each * count - rows), (0, 0))).astype(BF)
    pieces = lax.all_to_all(padded.reshape(count, each, LANES), "zh", 0, 0, tiled=True)
    piece = jnp.sum(pieces.astype(F32), axis=0).astype(BF)
    return lax.all_gather(piece, "zh", axis=0, tiled=True)[:rows]


def everywhere(part):
    return lax.all_to_all(jnp.broadcast_to(part[None], (PARTS, *part.shape)), NEAR, 0, 0, tiled=True)


def unspread_kernel(factor, w, img, txt):
    for t, out in enumerate((img, txt)):
        for k in range(WIDTH // LANES):
            for row, count, part, at in cut(t, k):
                out[row : row + count, k * LANES : (k + 1) * LANES] = (
                    w[part, at : at + count, :].astype(F32) * factor
                )


def body(img_embed, txt_embed, img_head, txt_head, pair_ids):
    groups = lax.axis_size(DP)
    me = lax.axis_index(DP)
    img_t, txt_t = img_embed.T, txt_embed.T

    def across(block):
        return swapped(block, "xh", 1)

    def adjacent(block):
        return lax.ppermute(block, ("xl", "xh"), [(i, i ^ 3) for i in range(4)])

    own = jnp.stack([img_t, txt_t])
    heads = jnp.stack([img_head, txt_head])
    far_z = swapped(own, "zh", lax.axis_size("zh") // 2)
    heads_x, own_x, far_y = adjacent(heads), across(own), swapped(own, "y", 1)
    far_y_x = lax.ppermute(own, ("y", "xh"), [(i, i ^ 3) for i in range(2 * lax.axis_size("y"))])
    table = pair_ids.reshape(groups, ROWS)
    places = [me, jnp.bitwise_xor(me, groups // 2), jnp.bitwise_xor(me, 1)]
    row_ids = jnp.concatenate([lax.dynamic_slice_in_dim(table, p, 1) for p in places])
    col_ids = row_ids[0][:, None]
    far_z, far_y_x, own_x, far_y, row_ids, col_ids = lax.optimization_barrier(
        (far_z, far_y_x, own_x, far_y, row_ids, col_ids)
    )
    near = jnp.stack([own, own_x, far_y, far_y_x])
    near_c = swapped(near, "c", 1)
    heads_c, heads_xc = swapped(heads, "c", 1), swapped(heads_x, "c", 1)
    far_x = across(far_z)
    far_c = swapped(far_z, "c", 1)

    big, half, line = ((WIDTH, ROWS), F32), ((WIDTH, ROWS), BF), ((1, ROWS), F32)
    rows = ((ROWS, WIDTH), BF)
    unit_flops = 2 * ROWS * WIDTH
    state = call(
        near_kernel,
        [((2, WIDTH, WIDTH), BF), big, big, rows, rows, big, big, line, line],
        [pltpu.VMEM((2, WIDTH, ROWS), F32), pltpu.VMEM(*half), pltpu.VMEM(*half)],
        unit_flops,
        [heads, heads_x, heads_c, heads_xc, near, near_c, col_ids, row_ids],
    )
    state, far_x = lax.optimization_barrier((state, far_x))
    far_z4 = [far_z, far_x, far_c, swapped(far_x, "c", 1)]
    img_grad, txt_grad, w = call(
        far_kernel,
        [((SHARD, ROWS), BF)] * 2 + [((PARTS, 2 * SPREAD // PARTS, LANES), BF)],
        [pltpu.VMEM(*s) for s in (big, half)],
        3 * unit_flops * (2 * WIDTH + 4 * ROWS + 4 * SHARD),
        [heads] + far_z4 + [img_t, txt_t, col_ids, row_ids] + list(state),
    )
    w = everywhere(summed_over_far(scattered(w)))
    factor = float(1.0 / np.sqrt(np.float32(groups * ROWS)))
    img_w, txt_w = pl.pallas_call(
        functools.partial(unspread_kernel, factor),
        out_shape=[jax.ShapeDtypeStruct((SHARD, WIDTH), F32)] * 2,
        compiler_params=pltpu.CompilerParams(vmem_limit_bytes=24 << 20),
    )(w)
    return img_grad.T, txt_grad.T, img_w, txt_w


def solution(mesh):
    fine = Mesh(mesh.devices.reshape(8, 2, 2, 4, 2, 2), DP + MP)
    return jax.shard_map(
        body,
        mesh=fine,
        in_specs=(P(DP, MP), P(DP, MP), P(MP, None), P(MP, None), P()),
        out_specs=(P(DP, MP), P(DP, MP), P(MP, None), P(MP, None)),
        check_vma=False,
    )
```

```python
import functools

import jax
import jax.numpy as jnp
import numpy as np
from jax import lax
from jax.experimental import pallas as pl
from jax.experimental.pallas import tpu as pltpu
from jax.sharding import Mesh, PartitionSpec as P

sharpness_multiplier = 10.0
sigmoid_shift_constant = -2.0
loss_scale = 32.0
epsilon = 1e-06
DP = ("zh", "zl", "xl", "y")
MP = ("xh", "c")
NEAR = ("zl", "xl", "y")
ROWS, WIDTH, SHARD, LANES = 384, 1152, 288, 128
PARTS = 16
SPREAD = 2816
BF, F32 = jnp.bfloat16, jnp.float32


def swapped(block, axis, bit):
    return lax.ppermute(block, axis, [(i, i ^ bit) for i in range(lax.axis_size(axis))])


def nn(a, b):
    return jnp.dot(a, b, preferred_element_type=F32)


def nt(a, b):
    return lax.dot_general(a, b, (((1,), (1,)), ((), ())), preferred_element_type=F32)


def joined(blocks, t):
    return jnp.concatenate([b[t] for b in blocks], axis=0)


def project(head, blocks, t, hid):
    hid[...] = nn(head[t], joined(blocks, t))


def norm_of(hid):
    return jnp.sqrt(jnp.sum(hid[...] * hid[...], axis=0, keepdims=True) + epsilon)


def grads_of(dots, same):
    z = sharpness_multiplier * dots + sigmoid_shift_constant
    s = 1.0 / (1.0 + jnp.exp(jnp.where(same, z, -z)))
    return (jnp.where(same, -loss_scale, loss_scale) * s).astype(BF)


def near_kernel(*refs):
    heads, (near, near_c, col_ids, row_ids) = refs[0:4], refs[4:8]
    turned, hid_i, hid_t, rows_i, rows_t, d_i, d_t, inv_i, inv_t = refs[8:17]
    hid, unit_i, unit_t = refs[17:]
    own = [r.at[k] for r in (near, near_c) for k in (0, 1)]
    far = [r.at[k] for r in (near, near_c) for k in (2, 3)]
    for t, (h, u, r, n) in enumerate(((hid_i, unit_i, rows_i, inv_i), (hid_t, unit_t, rows_t, inv_t))):
        turned[t] = joined(heads, t).T
        pair = nn(turned[t], jnp.concatenate([joined(own, t), joined(far, t)], axis=1))
        h[...] = pair[:, :ROWS]
        hid[t] = pair[:, ROWS:]
        n[...] = 1.0 / norm_of(h)
        u[...] = (h[...] * n[...]).astype(BF)
        r[...] = u[...].T
    g = grads_of(nn(rows_i[...], unit_t[...]), col_ids[...] == row_ids[0:1, :])
    d_i[...] = nt(unit_t[...], g)
    d_t[...] = nn(unit_i[...], g)
    same = col_ids[...] == row_ids[2:3, :]
    for t, (rows, unit, d) in enumerate(((rows_t, unit_t, d_t), (rows_i, unit_i, d_i))):
        unit[...] = (hid[t] * (1.0 / norm_of(hid.at[t]))).astype(BF)
        g = grads_of(nn(rows[...], unit[...]), same)
        d[...] += nt(unit[...], g)


def cut(tower, block, stop=0):
    piece, row = SPREAD // PARTS, block * SHARD
    stop = stop or row + SHARD
    while row < stop:
        part, inside = divmod(row, piece)
        count = min(piece - inside, stop - row)
        yield row - block * SHARD, count, part, tower * piece + inside
        row += count


def far_kernel(*refs):
    heads, far, img_embed, txt_embed, col_ids, row_ids = refs[0], refs[1:5], *refs[5:9]
    turned, hid_i, hid_t, rows_i, rows_t, d_i, d_t, inv_i, inv_t = refs[9:18]
    grad_i, grad_t, w, hid, unit = refs[18:]
    same = col_ids[...] == row_ids[1:2, :]
    order = (
        (0, rows_i, d_i, hid_i, inv_i, img_embed, grad_i),
        (1, rows_t, d_t, hid_t, inv_t, txt_embed, grad_t),
    )
    for tower, rows, d, h, n, embed, grad in order:
        project(turned, far, 1 - tower, hid)
        unit[...] = (hid[...] * (1.0 / norm_of(hid))).astype(BF)
        g = grads_of(nn(rows[...], unit[...]), same)
        full = sharpness_multiplier * (d[...] + nt(unit[...], g))
        scale = n[...]
        along = jnp.sum(h[...] * full, axis=0, keepdims=True) * (scale * scale)
        dhid = ((full - h[...] * along) * scale).astype(BF)
        total = nt(embed[...], dhid).astype(BF)
        for k in range(WIDTH // LANES):
            for row, count, part, at in cut(tower, k):
                w[part, at : at + count, :] = total[row : row + count, k * LANES : (k + 1) * LANES]
        for row, count, part, at in cut(tower, WIDTH // LANES, SPREAD):
            w[part, at : at + count, :] = jnp.zeros((count, LANES), BF)
        grad[...] = nn(heads[tower], dhid).astype(BF)


def call(kernel, out, scratch, flops, args):
    out = [jax.ShapeDtypeStruct(s, d) for s, d in out]
    size = sum(a.size * a.dtype.itemsize for a in args) + sum(o.size * o.dtype.itemsize for o in out)
    return pl.pallas_call(
        kernel,
        out_shape=out,
        in_specs=[pl.BlockSpec(memory_space=pltpu.VMEM)] * len(args),
        out_specs=[pl.BlockSpec(memory_space=pltpu.VMEM)] * len(out),
        scratch_shapes=scratch,
        compiler_params=pltpu.CompilerParams(vmem_limit_bytes=24 << 20),
        cost_estimate=pl.CostEstimate(flops=flops, bytes_accessed=size, transcendentals=ROWS * WIDTH),
    )(*args)


def scattered(w):
    parts = lax.all_to_all(w, NEAR, 0, 0, tiled=True)
    return jnp.sum(parts.astype(F32), axis=0)


def summed_over_far(part):
    count, rows = lax.axis_size("zh"), part.shape[0]
    each = -(-rows // (count * 8)) * 8
    padded = jnp.pad(part, ((0, each * count - rows), (0, 0))).astype(BF)
    pieces = lax.all_to_all(padded.reshape(count, each, LANES), "zh", 0, 0, tiled=True)
    piece = jnp.sum(pieces.astype(F32), axis=0).astype(BF)
    copies = jnp.broadcast_to(piece[None], (count, each, LANES))
    return lax.all_to_all(copies, "zh", 0, 0, tiled=True).reshape(count * each, LANES)[:rows]


def everywhere(part):
    return lax.all_to_all(jnp.broadcast_to(part[None], (PARTS, *part.shape)), NEAR, 0, 0, tiled=True)


def unspread_kernel(factor, w, img, txt):
    for t, out in enumerate((img, txt)):
        for k in range(WIDTH // LANES):
            for row, count, part, at in cut(t, k):
                out[row : row + count, k * LANES : (k + 1) * LANES] = (
                    w[part, at : at + count, :].astype(F32) * factor
                )


def body(img_embed, txt_embed, img_head, txt_head, pair_ids):
    groups = lax.axis_size(DP)
    me = lax.axis_index(DP)
    img_t, txt_t = img_embed.T, txt_embed.T

    def across(block):
        return swapped(block, "xh", 1)

    def adjacent(block):
        return lax.ppermute(block, ("xl", "xh"), [(i, i ^ 3) for i in range(4)])

    own = jnp.stack([img_t, txt_t])
    heads = jnp.stack([img_head, txt_head])
    far_z = swapped(own, "zh", lax.axis_size("zh") // 2)
    heads_x, own_x, far_y = adjacent(heads), across(own), swapped(own, "y", 1)
    far_y_x = lax.ppermute(own, ("y", "xh"), [(i, i ^ 3) for i in range(2 * lax.axis_size("y"))])
    table = pair_ids.reshape(groups, ROWS)
    places = [me, jnp.bitwise_xor(me, groups // 2), jnp.bitwise_xor(me, 1)]
    row_ids = jnp.concatenate([lax.dynamic_slice_in_dim(table, p, 1) for p in places])
    col_ids = row_ids[0][:, None]
    far_z, far_y_x, own_x, far_y, row_ids, col_ids = lax.optimization_barrier(
        (far_z, far_y_x, own_x, far_y, row_ids, col_ids)
    )
    near = jnp.stack([own, own_x, far_y, far_y_x])
    near_c = swapped(near, "c", 1)
    heads_c, heads_xc = swapped(heads, "c", 1), swapped(heads_x, "c", 1)
    far_x = across(far_z)
    far_c = swapped(far_z, "c", 1)

    big, half, line = ((WIDTH, ROWS), F32), ((WIDTH, ROWS), BF), ((1, ROWS), F32)
    rows = ((ROWS, WIDTH), BF)
    unit_flops = 2 * ROWS * WIDTH
    state = call(
        near_kernel,
        [((2, WIDTH, WIDTH), BF), big, big, rows, rows, big, big, line, line],
        [pltpu.VMEM((2, WIDTH, ROWS), F32), pltpu.VMEM(*half), pltpu.VMEM(*half)],
        unit_flops,
        [heads, heads_x, heads_c, heads_xc, near, near_c, col_ids, row_ids],
    )
    state, far_x = lax.optimization_barrier((state, far_x))
    far_z4 = [far_z, far_x, far_c, swapped(far_x, "c", 1)]
    img_grad, txt_grad, w = call(
        far_kernel,
        [((SHARD, ROWS), BF)] * 2 + [((PARTS, 2 * SPREAD // PARTS, LANES), BF)],
        [pltpu.VMEM(*s) for s in (big, half)],
        3 * unit_flops * (2 * WIDTH + 4 * ROWS + 4 * SHARD),
        [heads] + far_z4 + [img_t, txt_t, col_ids, row_ids] + list(state),
    )
    w = everywhere(summed_over_far(scattered(w)))
    factor = float(1.0 / np.sqrt(np.float32(groups * ROWS)))
    img_w, txt_w = pl.pallas_call(
        functools.partial(unspread_kernel, factor),
        out_shape=[jax.ShapeDtypeStruct((SHARD, WIDTH), F32)] * 2,
        compiler_params=pltpu.CompilerParams(vmem_limit_bytes=24 << 20),
    )(w)
    return img_grad.T, txt_grad.T, img_w, txt_w


def solution(mesh):
    fine = Mesh(mesh.devices.reshape(8, 2, 2, 4, 2, 2), DP + MP)
    return jax.shard_map(
        body,
        mesh=fine,
        in_specs=(P(DP, MP), P(DP, MP), P(MP, None), P(MP, None), P()),
        out_specs=(P(DP, MP), P(DP, MP), P(MP, None), P(MP, None)),
        check_vma=False,
    )
```

```python
import functools

import jax
import jax.numpy as jnp
import numpy as np
from jax import lax
from jax.experimental import pallas as pl
from jax.experimental.pallas import tpu as pltpu
from jax.sharding import Mesh, PartitionSpec as P

sharpness_multiplier = 10.0
sigmoid_shift_constant = -2.0
loss_scale = 32.0
epsilon = 1e-06
DP = ("zh", "zl", "xl", "y")
MP = ("xh", "c")
NEAR = ("zl", "xl", "y")
ROWS, WIDTH, SHARD, LANES = 384, 1152, 288, 128
PARTS = 16
SPREAD = 2816
BF, F32 = jnp.bfloat16, jnp.float32


def swapped(block, axis, bit):
    return lax.ppermute(block, axis, [(i, i ^ bit) for i in range(lax.axis_size(axis))])


def nn(a, b):
    return jnp.dot(a, b, preferred_element_type=F32)


def nt(a, b):
    return lax.dot_general(a, b, (((1,), (1,)), ((), ())), preferred_element_type=F32)


def joined(blocks, t):
    return jnp.concatenate([b[t] for b in blocks], axis=0)


def project(head, blocks, t, hid):
    hid[...] = nn(head[t], joined(blocks, t))


def norm_of(hid):
    return jnp.sqrt(jnp.sum(hid[...] * hid[...], axis=0, keepdims=True) + epsilon)


def grads_of(dots, same):
    z = sharpness_multiplier * dots + sigmoid_shift_constant
    s = 1.0 / (1.0 + jnp.exp(jnp.where(same, z, -z)))
    return (jnp.where(same, -loss_scale, loss_scale) * s).astype(BF)


def near_kernel(*refs):
    heads, (near, near_c, col_ids, row_ids) = refs[0:4], refs[4:8]
    turned, hid_i, hid_t, rows_i, rows_t, d_i, d_t, inv_i, inv_t = refs[8:17]
    hid, unit_i, unit_t = refs[17:]
    own = [r.at[k] for r in (near, near_c) for k in (0, 1)]
    far = [r.at[k] for r in (near, near_c) for k in (2, 3)]
    for t, (h, u, r, n) in enumerate(((hid_i, unit_i, rows_i, inv_i), (hid_t, unit_t, rows_t, inv_t))):
        turned[t] = joined(heads, t).T
        pair = nn(turned[t], jnp.concatenate([joined(own, t), joined(far, t)], axis=1))
        h[...] = pair[:, :ROWS]
        hid[t] = pair[:, ROWS:]
        n[...] = 1.0 / norm_of(h)
        u[...] = (h[...] * n[...]).astype(BF)
        r[...] = u[...].T
    g = grads_of(nn(rows_i[...], unit_t[...]), col_ids[...] == row_ids[0:1, :])
    d_i[...] = nt(unit_t[...], g)
    d_t[...] = nn(unit_i[...], g)
    same = col_ids[...] == row_ids[2:3, :]
    for t, (rows, unit, d) in enumerate(((rows_t, unit_t, d_t), (rows_i, unit_i, d_i))):
        unit[...] = (hid[t] * (1.0 / norm_of(hid.at[t]))).astype(BF)
        g = grads_of(nn(rows[...], unit[...]), same)
        d[...] += nt(unit[...], g)


def cut(tower, block, stop=0):
    piece, row = SPREAD // PARTS, block * SHARD
    stop = stop or row + SHARD
    while row < stop:
        part, inside = divmod(row, piece)
        count = min(piece - inside, stop - row)
        yield row - block * SHARD, count, part, tower * piece + inside
        row += count


def far_kernel(*refs):
    heads, far, img_embed, txt_embed, col_ids, row_ids = refs[0], refs[1:5], *refs[5:9]
    turned, hid_i, hid_t, rows_i, rows_t, d_i, d_t, inv_i, inv_t = refs[9:18]
    grad_i, grad_t, w, hid, unit = refs[18:]
    same = col_ids[...] == row_ids[1:2, :]
    order = (
        (0, rows_i, d_i, hid_i, inv_i, img_embed, grad_i),
        (1, rows_t, d_t, hid_t, inv_t, txt_embed, grad_t),
    )
    for tower, rows, d, h, n, embed, grad in order:
        project(turned, far, 1 - tower, hid)
        unit[...] = (hid[...] * (1.0 / norm_of(hid))).astype(BF)
        g = grads_of(nn(rows[...], unit[...]), same)
        full = sharpness_multiplier * (d[...] + nt(unit[...], g))
        scale = n[...]
        along = jnp.sum(h[...] * full, axis=0, keepdims=True) * (scale * scale)
        dhid = ((full - h[...] * along) * scale).astype(BF)
        total = nt(embed[...], dhid).astype(BF)
        for k in range(WIDTH // LANES):
            for row, count, part, at in cut(tower, k):
                w[part, at : at + count, :] = total[row : row + count, k * LANES : (k + 1) * LANES]
        for row, count, part, at in cut(tower, WIDTH // LANES, SPREAD):
            w[part, at : at + count, :] = jnp.zeros((count, LANES), BF)
        grad[...] = nn(heads[tower], dhid).astype(BF)


def call(kernel, out, scratch, flops, args):
    out = [jax.ShapeDtypeStruct(s, d) for s, d in out]
    size = sum(a.size * a.dtype.itemsize for a in args) + sum(o.size * o.dtype.itemsize for o in out)
    return pl.pallas_call(
        kernel,
        out_shape=out,
        in_specs=[pl.BlockSpec(memory_space=pltpu.VMEM)] * len(args),
        out_specs=[pl.BlockSpec(memory_space=pltpu.VMEM)] * len(out),
        scratch_shapes=scratch,
        compiler_params=pltpu.CompilerParams(vmem_limit_bytes=24 << 20),
        cost_estimate=pl.CostEstimate(flops=flops, bytes_accessed=size, transcendentals=ROWS * WIDTH),
    )(*args)


def scattered(w):
    parts = lax.all_to_all(w, NEAR, 0, 0, tiled=True)
    return jnp.sum(parts.astype(F32), axis=0)


def summed_over_far(part):
    count, rows = lax.axis_size("zh"), part.shape[0]
    each = -(-rows // (count * 8)) * 8
    padded = jnp.pad(part, ((0, each * count - rows), (0, 0))).astype(BF)
    pieces = lax.all_to_all(padded.reshape(count, each, LANES), "zh", 0, 0, tiled=True)
    piece = jnp.sum(pieces.astype(F32), axis=0).astype(BF)
    copies = jnp.broadcast_to(piece[None], (count, each, LANES))
    return lax.all_to_all(copies, "zh", 0, 0, tiled=True).reshape(count * each, LANES)[:rows]


def everywhere(part):
    return lax.all_to_all(jnp.broadcast_to(part[None], (PARTS, *part.shape)), NEAR, 0, 0, tiled=True)


def unspread_kernel(factor, w, img, txt):
    for t, out in enumerate((img, txt)):
        for k in range(WIDTH // LANES):
            for row, count, part, at in cut(t, k):
                out[row : row + count, k * LANES : (k + 1) * LANES] = (
                    w[part, at : at + count, :].astype(F32) * factor
                )


def body(img_embed, txt_embed, img_head, txt_head, pair_ids):
    groups = lax.axis_size(DP)
    me = lax.axis_index(DP)
    img_t, txt_t = img_embed.T, txt_embed.T

    def across(block):
        return swapped(block, "xh", 1)

    def adjacent(block):
        return lax.ppermute(block, ("xl", "xh"), [(i, i ^ 3) for i in range(4)])

    def along_z(block, hops):
        axes = ("zh", "zl")
        count = lax.axis_size(axes)
        return lax.ppermute(block, axes, [(i, (i + hops) % count) for i in range(count)])

    most = lax.axis_size(("zh", "zl")) // 2 - 1
    own = jnp.stack([img_t, txt_t])
    heads = jnp.stack([img_head, txt_head])
    far_i, far_t = along_z(img_t, most), along_z(txt_t, -most)
    heads_x, own_x, far_y = adjacent(heads), across(own), swapped(own, "y", 1)
    far_i, far_t, far_y_x = along_z(far_i, 1), along_z(far_t, -1), swapped(own_x, "y", 1)
    table = pair_ids.reshape(groups, ROWS)
    places = [me, jnp.bitwise_xor(me, groups // 2), jnp.bitwise_xor(me, 1)]
    row_ids = jnp.concatenate([lax.dynamic_slice_in_dim(table, p, 1) for p in places])
    col_ids = row_ids[0][:, None]
    far_i, far_t, far_y, far_y_x, heads_x, row_ids, col_ids = lax.optimization_barrier(
        (far_i, far_t, far_y, far_y_x, heads_x, row_ids, col_ids)
    )
    far_z = jnp.stack([far_i, far_t])
    near = jnp.stack([own, own_x, far_y, far_y_x])
    near_c = swapped(near, "c", 1)
    heads_c, heads_xc = swapped(heads, "c", 1), swapped(heads_x, "c", 1)
    far_x = across(far_z)
    far_c = swapped(far_z, "c", 1)

    big, half, line = ((WIDTH, ROWS), F32), ((WIDTH, ROWS), BF), ((1, ROWS), F32)
    rows = ((ROWS, WIDTH), BF)
    unit_flops = 2 * ROWS * WIDTH
    state = call(
        near_kernel,
        [((2, WIDTH, WIDTH), BF), big, big, rows, rows, big, big, line, line],
        [pltpu.VMEM((2, WIDTH, ROWS), F32), pltpu.VMEM(*half), pltpu.VMEM(*half)],
        unit_flops,
        [heads, heads_x, heads_c, heads_xc, near, near_c, col_ids, row_ids],
    )
    state, far_x = lax.optimization_barrier((state, far_x))
    far_z4 = [far_z, far_x, far_c, swapped(far_x, "c", 1)]
    img_grad, txt_grad, w = call(
        far_kernel,
        [((SHARD, ROWS), BF)] * 2 + [((PARTS, 2 * SPREAD // PARTS, LANES), BF)],
        [pltpu.VMEM(*s) for s in (big, half)],
        3 * unit_flops * (2 * WIDTH + 4 * ROWS + 4 * SHARD),
        [heads] + far_z4 + [img_t, txt_t, col_ids, row_ids] + list(state),
    )
    w = everywhere(summed_over_far(scattered(w)))
    factor = float(1.0 / np.sqrt(np.float32(groups * ROWS)))
    img_w, txt_w = pl.pallas_call(
        functools.partial(unspread_kernel, factor),
        out_shape=[jax.ShapeDtypeStruct((SHARD, WIDTH), F32)] * 2,
        compiler_params=pltpu.CompilerParams(vmem_limit_bytes=24 << 20),
    )(w)
    return img_grad.T, txt_grad.T, img_w, txt_w


def solution(mesh):
    fine = Mesh(mesh.devices.reshape(8, 2, 2, 4, 2, 2), DP + MP)
    return jax.shard_map(
        body,
        mesh=fine,
        in_specs=(P(DP, MP), P(DP, MP), P(MP, None), P(MP, None), P()),
        out_specs=(P(DP, MP), P(DP, MP), P(MP, None), P(MP, None)),
        check_vma=False,
    )
```

```python
import functools

import jax
import jax.numpy as jnp
import numpy as np
from jax import lax
from jax.experimental import pallas as pl
from jax.experimental.pallas import tpu as pltpu
from jax.sharding import Mesh, PartitionSpec as P

sharpness_multiplier = 10.0
sigmoid_shift_constant = -2.0
loss_scale = 32.0
epsilon = 1e-06
DP = ("zh", "zl", "xl", "y")
MP = ("xh", "c")
NEAR = ("zl", "xl", "y")
ROWS, WIDTH, SHARD, LANES = 384, 1152, 288, 128
PARTS = 16
SPREAD = 2816
BF, F32 = jnp.bfloat16, jnp.float32


def swapped(block, axis, bit):
    return lax.ppermute(block, axis, [(i, i ^ bit) for i in range(lax.axis_size(axis))])


def nn(a, b):
    return jnp.dot(a, b, preferred_element_type=F32)


def nt(a, b):
    return lax.dot_general(a, b, (((1,), (1,)), ((), ())), preferred_element_type=F32)


def joined(blocks, t):
    return jnp.concatenate([b[t] for b in blocks], axis=0)


def project(head, blocks, t, hid):
    hid[...] = nn(head[t], joined(blocks, t))


def norm_of(hid):
    return jnp.sqrt(jnp.sum(hid[...] * hid[...], axis=0, keepdims=True) + epsilon)


def grads_of(dots, same):
    z = sharpness_multiplier * dots + sigmoid_shift_constant
    s = 1.0 / (1.0 + jnp.exp(jnp.where(same, z, -z)))
    return (jnp.where(same, -loss_scale, loss_scale) * s).astype(BF)


def near_kernel(*refs):
    heads, (near, near_c, col_ids, row_ids) = refs[0:4], refs[4:8]
    turned, hid_i, hid_t, rows_i, rows_t, d_i, d_t, inv_i, inv_t = refs[8:17]
    hid, unit_i, unit_t = refs[17:]
    own = [r.at[k] for r in (near, near_c) for k in (0, 1)]
    far = [r.at[k] for r in (near, near_c) for k in (2, 3)]
    for t, (h, u, r, n) in enumerate(((hid_i, unit_i, rows_i, inv_i), (hid_t, unit_t, rows_t, inv_t))):
        turned[t] = joined(heads, t).T
        pair = nn(turned[t], jnp.concatenate([joined(own, t), joined(far, t)], axis=1))
        h[...] = pair[:, :ROWS]
        hid[t] = pair[:, ROWS:]
        n[...] = 1.0 / norm_of(h)
        u[...] = (h[...] * n[...]).astype(BF)
        r[...] = u[...].T
    g = grads_of(nn(rows_i[...], unit_t[...]), col_ids[...] == row_ids[0:1, :])
    d_i[...] = nt(unit_t[...], g)
    d_t[...] = nn(unit_i[...], g)
    same = col_ids[...] == row_ids[2:3, :]
    for t, (rows, unit, d) in enumerate(((rows_t, unit_t, d_t), (rows_i, unit_i, d_i))):
        unit[...] = (hid[t] * (1.0 / norm_of(hid.at[t]))).astype(BF)
        g = grads_of(nn(rows[...], unit[...]), same)
        d[...] += nt(unit[...], g)


def cut(tower, block, stop=0):
    piece, row = SPREAD // PARTS, block * SHARD
    stop = stop or row + SHARD
    while row < stop:
        part, inside = divmod(row, piece)
        count = min(piece - inside, stop - row)
        yield row - block * SHARD, count, part, tower * piece + inside
        row += count


def far_kernel(*refs):
    heads, far, img_embed, txt_embed, col_ids, row_ids = refs[0], refs[1:5], *refs[5:9]
    turned, hid_i, hid_t, rows_i, rows_t, d_i, d_t, inv_i, inv_t = refs[9:18]
    grad_i, grad_t, w, hid, unit = refs[18:]
    same = col_ids[...] == row_ids[1:2, :]
    order = (
        (0, rows_i, d_i, hid_i, inv_i, img_embed, grad_i),
        (1, rows_t, d_t, hid_t, inv_t, txt_embed, grad_t),
    )
    for tower, rows, d, h, n, embed, grad in order:
        project(turned, far, 1 - tower, hid)
        unit[...] = (hid[...] * (1.0 / norm_of(hid))).astype(BF)
        g = grads_of(nn(rows[...], unit[...]), same)
        full = sharpness_multiplier * (d[...] + nt(unit[...], g))
        scale = n[...]
        along = jnp.sum(h[...] * full, axis=0, keepdims=True) * (scale * scale)
        dhid = ((full - h[...] * along) * scale).astype(BF)
        total = nt(embed[...], dhid).astype(BF)
        for k in range(WIDTH // LANES):
            for row, count, part, at in cut(tower, k):
                w[part, at : at + count, :] = total[row : row + count, k * LANES : (k + 1) * LANES]
        for row, count, part, at in cut(tower, WIDTH // LANES, SPREAD):
            w[part, at : at + count, :] = jnp.zeros((count, LANES), BF)
        grad[...] = nn(heads[tower], dhid).astype(BF)


def call(kernel, out, scratch, flops, args):
    out = [jax.ShapeDtypeStruct(s, d) for s, d in out]
    size = sum(a.size * a.dtype.itemsize for a in args) + sum(o.size * o.dtype.itemsize for o in out)
    return pl.pallas_call(
        kernel,
        out_shape=out,
        in_specs=[pl.BlockSpec(memory_space=pltpu.VMEM)] * len(args),
        out_specs=[pl.BlockSpec(memory_space=pltpu.VMEM)] * len(out),
        scratch_shapes=scratch,
        compiler_params=pltpu.CompilerParams(vmem_limit_bytes=24 << 20),
        cost_estimate=pl.CostEstimate(flops=flops, bytes_accessed=size, transcendentals=ROWS * WIDTH),
    )(*args)


def copy_kernel(source, target):
    target[...] = source[...]


def handed_on(block, flops):
    return pl.pallas_call(
        copy_kernel,
        out_shape=jax.ShapeDtypeStruct(block.shape, block.dtype),
        cost_estimate=pl.CostEstimate(flops=flops, bytes_accessed=2 * block.size * 2, transcendentals=0),
    )(block)


def scattered(w):
    parts = lax.all_to_all(w, NEAR, 0, 0, tiled=True)
    return jnp.sum(parts.astype(F32), axis=0)


def summed_over_far(part):
    count, rows = lax.axis_size("zh"), part.shape[0]
    each = -(-rows // (count * 8)) * 8
    padded = jnp.pad(part, ((0, each * count - rows), (0, 0))).astype(BF)
    pieces = lax.all_to_all(padded.reshape(count, each, LANES), "zh", 0, 0, tiled=True)
    piece = jnp.sum(pieces.astype(F32), axis=0).astype(BF)
    copies = jnp.broadcast_to(piece[None], (count, each, LANES))
    return lax.all_to_all(copies, "zh", 0, 0, tiled=True).reshape(count * each, LANES)[:rows]


def everywhere(part):
    return lax.all_to_all(jnp.broadcast_to(part[None], (PARTS, *part.shape)), NEAR, 0, 0, tiled=True)


def unspread_kernel(factor, w, img, txt):
    for t, out in enumerate((img, txt)):
        for k in range(WIDTH // LANES):
            for row, count, part, at in cut(t, k):
                out[row : row + count, k * LANES : (k + 1) * LANES] = (
                    w[part, at : at + count, :].astype(F32) * factor
                )


def body(img_embed, txt_embed, img_head, txt_head, pair_ids):
    groups = lax.axis_size(DP)
    me = lax.axis_index(DP)
    img_t, txt_t = img_embed.T, txt_embed.T

    def across(block):
        return swapped(block, "xh", 1)

    def adjacent(block):
        return lax.ppermute(block, ("xl", "xh"), [(i, i ^ 3) for i in range(4)])

    own = jnp.stack([img_t, txt_t])
    heads = jnp.stack([img_head, txt_head])
    far_z = swapped(own, "zh", lax.axis_size("zh") // 2)
    heads_x, own_x, far_y = adjacent(heads), across(own), swapped(own, "y", 1)
    far_y_x = lax.ppermute(own, ("y", "xh"), [(i, i ^ 3) for i in range(2 * lax.axis_size("y"))])
    table = pair_ids.reshape(groups, ROWS)
    places = [me, jnp.bitwise_xor(me, groups // 2), jnp.bitwise_xor(me, 1)]
    row_ids = jnp.concatenate([lax.dynamic_slice_in_dim(table, p, 1) for p in places])
    col_ids = row_ids[0][:, None]
    far_y_x, own_x, far_y, row_ids, col_ids = lax.optimization_barrier(
        (far_y_x, own_x, far_y, row_ids, col_ids)
    )
    near = jnp.stack([own, own_x, far_y, far_y_x])
    near_c = swapped(near, "c", 1)
    heads_c, heads_xc = swapped(heads, "c", 1), swapped(heads_x, "c", 1)
    far_z = handed_on(far_z, 20 * 10**9)
    far_x = across(far_z)
    far_c = swapped(far_z, "c", 1)

    big, half, line = ((WIDTH, ROWS), F32), ((WIDTH, ROWS), BF), ((1, ROWS), F32)
    rows = ((ROWS, WIDTH), BF)
    unit_flops = 2 * ROWS * WIDTH
    state = call(
        near_kernel,
        [((2, WIDTH, WIDTH), BF), big, big, rows, rows, big, big, line, line],
        [pltpu.VMEM((2, WIDTH, ROWS), F32), pltpu.VMEM(*half), pltpu.VMEM(*half)],
        unit_flops,
        [heads, heads_x, heads_c, heads_xc, near, near_c, col_ids, row_ids],
    )
    state, far_x = lax.optimization_barrier((state, far_x))
    far_z4 = [far_z, far_x, far_c, swapped(far_x, "c", 1)]
    img_grad, txt_grad, w = call(
        far_kernel,
        [((SHARD, ROWS), BF)] * 2 + [((PARTS, 2 * SPREAD // PARTS, LANES), BF)],
        [pltpu.VMEM(*s) for s in (big, half)],
        3 * unit_flops * (2 * WIDTH + 4 * ROWS + 4 * SHARD),
        [heads] + far_z4 + [img_t, txt_t, col_ids, row_ids] + list(state),
    )
    w = everywhere(summed_over_far(scattered(w)))
    factor = float(1.0 / np.sqrt(np.float32(groups * ROWS)))
    img_w, txt_w = pl.pallas_call(
        functools.partial(unspread_kernel, factor),
        out_shape=[jax.ShapeDtypeStruct((SHARD, WIDTH), F32)] * 2,
        compiler_params=pltpu.CompilerParams(vmem_limit_bytes=24 << 20),
    )(w)
    return img_grad.T, txt_grad.T, img_w, txt_w


def solution(mesh):
    fine = Mesh(mesh.devices.reshape(8, 2, 2, 4, 2, 2), DP + MP)
    return jax.shard_map(
        body,
        mesh=fine,
        in_specs=(P(DP, MP), P(DP, MP), P(MP, None), P(MP, None), P()),
        out_specs=(P(DP, MP), P(DP, MP), P(MP, None), P(MP, None)),
        check_vma=False,
    )
```

```python
import functools

import jax
import jax.numpy as jnp
import numpy as np
from jax import lax
from jax.experimental import pallas as pl
from jax.experimental.pallas import tpu as pltpu
from jax.sharding import Mesh, PartitionSpec as P

sharpness_multiplier = 10.0
sigmoid_shift_constant = -2.0
loss_scale = 32.0
epsilon = 1e-06
DP = ("zh", "zl", "xl", "y")
MP = ("xh", "c")
NEAR = ("zl", "xl", "y")
ROWS, WIDTH, SHARD, LANES = 384, 1152, 288, 128
PARTS = 16
SPREAD = 2816
BF, F32 = jnp.bfloat16, jnp.float32


def swapped(block, axis, bit):
    return lax.ppermute(block, axis, [(i, i ^ bit) for i in range(lax.axis_size(axis))])


def nn(a, b):
    return jnp.dot(a, b, preferred_element_type=F32)


def nt(a, b):
    return lax.dot_general(a, b, (((1,), (1,)), ((), ())), preferred_element_type=F32)


def joined(blocks, t):
    return jnp.concatenate([b[t] for b in blocks], axis=0)


def project(head, blocks, t, hid):
    hid[...] = nn(head[t], joined(blocks, t))


def norm_of(hid):
    return jnp.sqrt(jnp.sum(hid[...] * hid[...], axis=0, keepdims=True) + epsilon)


def grads_of(dots, same):
    z = sharpness_multiplier * dots + sigmoid_shift_constant
    s = 1.0 / (1.0 + jnp.exp(jnp.where(same, z, -z)))
    return (jnp.where(same, -loss_scale, loss_scale) * s).astype(BF)


def near_kernel(*refs):
    heads, (near, near_c, col_ids, row_ids) = refs[0:4], refs[4:8]
    turned, hid_i, hid_t, rows_i, rows_t, d_i, d_t, inv_i, inv_t = refs[8:17]
    hid, unit_i, unit_t = refs[17:]
    own = [r.at[k] for r in (near, near_c) for k in (0, 1)]
    far = [r.at[k] for r in (near, near_c) for k in (2, 3)]
    for t, (h, u, r, n) in enumerate(((hid_i, unit_i, rows_i, inv_i), (hid_t, unit_t, rows_t, inv_t))):
        turned[t] = joined(heads, t).T
        pair = nn(turned[t], jnp.concatenate([joined(own, t), joined(far, t)], axis=1))
        h[...] = pair[:, :ROWS]
        hid[t] = pair[:, ROWS:]
        n[...] = 1.0 / norm_of(h)
        u[...] = (h[...] * n[...]).astype(BF)
        r[...] = u[...].T
    g = grads_of(nn(rows_i[...], unit_t[...]), col_ids[...] == row_ids[0:1, :])
    d_i[...] = nt(unit_t[...], g)
    d_t[...] = nn(unit_i[...], g)
    same = col_ids[...] == row_ids[2:3, :]
    for t, (rows, unit, d) in enumerate(((rows_t, unit_t, d_t), (rows_i, unit_i, d_i))):
        unit[...] = (hid[t] * (1.0 / norm_of(hid.at[t]))).astype(BF)
        g = grads_of(nn(rows[...], unit[...]), same)
        d[...] += nt(unit[...], g)


def cut(tower, block, stop=0):
    piece, row = SPREAD // PARTS, block * SHARD
    stop = stop or row + SHARD
    while row < stop:
        part, inside = divmod(row, piece)
        count = min(piece - inside, stop - row)
        yield row - block * SHARD, count, part, tower * piece + inside
        row += count


def far_kernel(*refs):
    heads, far, img_embed, txt_embed, col_ids, row_ids = refs[0], refs[1:5], *refs[5:9]
    turned, hid_i, hid_t, rows_i, rows_t, d_i, d_t, inv_i, inv_t = refs[9:18]
    dhid_i, dhid_t, w, hid, unit = refs[18:]
    same = col_ids[...] == row_ids[1:2, :]
    order = (
        (0, rows_i, d_i, hid_i, inv_i, img_embed, dhid_i),
        (1, rows_t, d_t, hid_t, inv_t, txt_embed, dhid_t),
    )
    for tower, rows, d, h, n, embed, kept in order:
        project(turned, far, 1 - tower, hid)
        unit[...] = (hid[...] * (1.0 / norm_of(hid))).astype(BF)
        g = grads_of(nn(rows[...], unit[...]), same)
        full = sharpness_multiplier * (d[...] + nt(unit[...], g))
        scale = n[...]
        along = jnp.sum(h[...] * full, axis=0, keepdims=True) * (scale * scale)
        dhid = ((full - h[...] * along) * scale).astype(BF)
        total = nt(embed[...], dhid).astype(BF)
        for k in range(WIDTH // LANES):
            for row, count, part, at in cut(tower, k):
                w[part, at : at + count, :] = total[row : row + count, k * LANES : (k + 1) * LANES]
        for row, count, part, at in cut(tower, WIDTH // LANES, SPREAD):
            w[part, at : at + count, :] = jnp.zeros((count, LANES), BF)
        kept[...] = dhid


def grad_kernel(heads, dhid_i, dhid_t, grad_i, grad_t):
    grad_i[...] = nn(heads[0], dhid_i[...]).astype(BF)
    grad_t[...] = nn(heads[1], dhid_t[...]).astype(BF)


def call(kernel, out, scratch, flops, args):
    out = [jax.ShapeDtypeStruct(s, d) for s, d in out]
    size = sum(a.size * a.dtype.itemsize for a in args) + sum(o.size * o.dtype.itemsize for o in out)
    return pl.pallas_call(
        kernel,
        out_shape=out,
        in_specs=[pl.BlockSpec(memory_space=pltpu.VMEM)] * len(args),
        out_specs=[pl.BlockSpec(memory_space=pltpu.VMEM)] * len(out),
        scratch_shapes=scratch,
        compiler_params=pltpu.CompilerParams(vmem_limit_bytes=24 << 20),
        cost_estimate=pl.CostEstimate(flops=flops, bytes_accessed=size, transcendentals=ROWS * WIDTH),
    )(*args)


def scattered(w):
    parts = lax.all_to_all(w, NEAR, 0, 0, tiled=True)
    return jnp.sum(parts.astype(F32), axis=0)


def summed_over_far(part):
    count, rows = lax.axis_size("zh"), part.shape[0]
    each = -(-rows // (count * 8)) * 8
    padded = jnp.pad(part, ((0, each * count - rows), (0, 0))).astype(BF)
    pieces = lax.all_to_all(padded.reshape(count, each, LANES), "zh", 0, 0, tiled=True)
    piece = jnp.sum(pieces.astype(F32), axis=0).astype(BF)
    copies = jnp.broadcast_to(piece[None], (count, each, LANES))
    return lax.all_to_all(copies, "zh", 0, 0, tiled=True).reshape(count * each, LANES)[:rows]


def everywhere(part):
    return lax.all_to_all(jnp.broadcast_to(part[None], (PARTS, *part.shape)), NEAR, 0, 0, tiled=True)


def unspread_kernel(factor, w, img, txt):
    for t, out in enumerate((img, txt)):
        for k in range(WIDTH // LANES):
            for row, count, part, at in cut(t, k):
                out[row : row + count, k * LANES : (k + 1) * LANES] = (
                    w[part, at : at + count, :].astype(F32) * factor
                )


def body(img_embed, txt_embed, img_head, txt_head, pair_ids):
    groups = lax.axis_size(DP)
    me = lax.axis_index(DP)
    img_t, txt_t = img_embed.T, txt_embed.T

    def across(block):
        return swapped(block, "xh", 1)

    def adjacent(block):
        return lax.ppermute(block, ("xl", "xh"), [(i, i ^ 3) for i in range(4)])

    own = jnp.stack([img_t, txt_t])
    heads = jnp.stack([img_head, txt_head])
    far_z = swapped(own, "zh", lax.axis_size("zh") // 2)
    heads_x, own_x, far_y = adjacent(heads), across(own), swapped(own, "y", 1)
    far_y_x = lax.ppermute(own, ("y", "xh"), [(i, i ^ 3) for i in range(2 * lax.axis_size("y"))])
    table = pair_ids.reshape(groups, ROWS)
    places = [me, jnp.bitwise_xor(me, groups // 2), jnp.bitwise_xor(me, 1)]
    row_ids = jnp.concatenate([lax.dynamic_slice_in_dim(table, p, 1) for p in places])
    col_ids = row_ids[0][:, None]
    far_z, far_y_x, own_x, far_y, row_ids, col_ids = lax.optimization_barrier(
        (far_z, far_y_x, own_x, far_y, row_ids, col_ids)
    )
    near = jnp.stack([own, own_x, far_y, far_y_x])
    near_c = swapped(near, "c", 1)
    heads_c, heads_xc = swapped(heads, "c", 1), swapped(heads_x, "c", 1)
    far_x = across(far_z)
    far_c = swapped(far_z, "c", 1)

    big, half, line = ((WIDTH, ROWS), F32), ((WIDTH, ROWS), BF), ((1, ROWS), F32)
    rows = ((ROWS, WIDTH), BF)
    unit_flops = 2 * ROWS * WIDTH
    state = call(
        near_kernel,
        [((2, WIDTH, WIDTH), BF), big, big, rows, rows, big, big, line, line],
        [pltpu.VMEM((2, WIDTH, ROWS), F32), pltpu.VMEM(*half), pltpu.VMEM(*half)],
        unit_flops,
        [heads, heads_x, heads_c, heads_xc, near, near_c, col_ids, row_ids],
    )
    state, far_x = lax.optimization_barrier((state, far_x))
    far_z4 = [far_z, far_x, far_c, swapped(far_x, "c", 1)]
    dhid_i, dhid_t, w = call(
        far_kernel,
        [half] * 2 + [((PARTS, 2 * SPREAD // PARTS, LANES), BF)],
        [pltpu.VMEM(*s) for s in (big, half)],
        3 * unit_flops * (2 * WIDTH + 4 * ROWS + 4 * SHARD),
        [heads] + far_z4 + [img_t, txt_t, col_ids, row_ids] + list(state),
    )
    img_grad, txt_grad = call(
        grad_kernel, [((SHARD, ROWS), BF)] * 2, [], 4 * unit_flops * SHARD, [heads, dhid_i, dhid_t]
    )
    w = everywhere(summed_over_far(scattered(w)))
    factor = float(1.0 / np.sqrt(np.float32(groups * ROWS)))
    img_w, txt_w = pl.pallas_call(
        functools.partial(unspread_kernel, factor),
        out_shape=[jax.ShapeDtypeStruct((SHARD, WIDTH), F32)] * 2,
        compiler_params=pltpu.CompilerParams(vmem_limit_bytes=24 << 20),
    )(w)
    return img_grad.T, txt_grad.T, img_w, txt_w


def solution(mesh):
    fine = Mesh(mesh.devices.reshape(8, 2, 2, 4, 2, 2), DP + MP)
    return jax.shard_map(
        body,
        mesh=fine,
        in_specs=(P(DP, MP), P(DP, MP), P(MP, None), P(MP, None), P()),
        out_specs=(P(DP, MP), P(DP, MP), P(MP, None), P(MP, None)),
        check_vma=False,
    )
```
